32 devices in a mesh: parts: 2 (over y), dp: 4 (over z), tensor: 4 (over x, core).
Axes of the slice: x: 2, y: 2, z: 4, core: 2. Of those that a mesh axis runs over, the one named last changes fastest.
Arguments:
- acts: bfloat16 [5632, 8192], P(('parts', 'dp'), 'tensor'), parts along dimension 0, may hold values from -6 to 6
- output_weight: bfloat16 [8192, 8192], P('tensor'), may hold values from -0.09375 to 0.09375
- adapter_down_weight: bfloat16 [384, 16, 8192], P('dp', None, 'tensor'), may hold values from -0.0625 to 0.0625
- adapter_up_weight: bfloat16 [384, 16, 8192], P('dp', None, 'tensor'), may hold values from -1.5 to 1.5
- segment_block_count: int32 [8, 16], P(('parts', 'dp')), parts along dimension 0, may hold values from 1 to 11, 44 in all within a row
- segment_adapter_id: int32 [8, 16], P(('parts', 'dp')), parts along dimension 0, may hold values from 0 to 383, as said below
- adapter_store_row: int32 [768], P('parts'), parts along dimension 0, may hold values from 0 to 383, as said below
Outputs:
- projected: bfloat16 [5632, 8192], P(('parts', 'dp'), 'tensor'), parts along dimension 0
The draws below stay inside these ranges and needn't reach their ends.
There are 2 independent parts, one for each index of `parts`. The reference program is written for one: setup_inputs(seed, part) draws one part's arguments, and reference() takes and returns one part's arrays. A program takes and returns all parts, laid end to end along the dimension named above; an argument that names none is the same for every part. Nothing has to cross between parts.
Inputs may be any that keep to these rules, and one draw needn't show every extreme that they name: `segment_adapter_id`: in each group, at most 5 segments name adapters whose slots lie in one block of 96 consecutive rows, and exactly 5 for some block. `adapter_store_row`: A permutation of 0 to 383.
All inputs are finite; a program needn't handle non-finite values.
Results may differ from the reference program's by a relative error of at most 0.012.
Values may be sent and summed in bfloat16 or wider, within the bound.
No kernel may reach another device: no remote copies, remote signals or barrier semaphores. Data moves between devices by JAX's collectives and lax.ppermute only.
A program may use at most 256 MiB of HBM per device.

```python
import math
import jax
import jax.numpy as jnp
import numpy as np
from jax import lax

MODEL_WIDTH = 8192
ADAPTER_RANK = 16
ADAPTER_TOTAL = 384
GROUP_SEGMENTS = 16
TOK = 704
TOKENS = 2816
MOST_BLOCKS = 11
N_DP = 4
N_TENSOR = 4


def shared_maps(key):
    slots = jax.random.permutation(jax.random.fold_in(key, 11), ADAPTER_TOTAL).astype(jnp.int32)
    inverse = jnp.zeros((ADAPTER_TOTAL,), jnp.int32).at[slots].set(jnp.arange(ADAPTER_TOTAL, dtype=jnp.int32))
    per_owner = ADAPTER_TOTAL // N_DP
    slots_cap = GROUP_SEGMENTS // N_DP + 1

    def one_group(group_key):
        first, second, third = jax.random.split(group_key, 3)
        order = jax.random.permutation(first, N_DP).astype(jnp.int32)
        owners = order[jnp.arange(GROUP_SEGMENTS, dtype=jnp.int32) // slots_cap]
        owners = owners[jax.random.permutation(second, GROUP_SEGMENTS)]
        within = jax.random.randint(third, (GROUP_SEGMENTS,), 0, per_owner, dtype=jnp.int32)
        return inverse[owners * per_owner + within]
    adapters = jax.vmap(one_group)(jax.random.split(jax.random.fold_in(key, 12), N_DP))
    return (slots, adapters)


def draw_adapter_store_row(key, part):
    slots, adapters = shared_maps(key)
    return slots


def draw_segment_adapter_id(key, part):
    slots, adapters = shared_maps(key)
    return adapters


def spiked(entries, own_key, source, target, blocks, factor):
    owner, partner = [(jnp.arange(entries.shape[position]) // (entries.shape[position] // blocks)).reshape([-1 if axis == position else 1 for axis in range(entries.ndim)]) for position in (source, target)]
    chosen = jax.random.permutation(own_key, blocks)[partner]
    strong = (owner == chosen) | (owner == (partner + blocks // 2) % blocks)
    return jnp.where(strong, factor * entries, entries)


def level_of(stream_key, dims, pieces, low, high):
    loudness = 1.0
    for axis_at, shards_of in pieces:
        steps = jax.random.uniform(jax.random.fold_in(jax.random.fold_in(stream_key, 6), axis_at), (shards_of,), jnp.float32, low / len(pieces), high / len(pieces))
        loudness = loudness * jnp.repeat(jnp.exp(steps), dims[axis_at] // shards_of).reshape((-1,) + (1,) * (len(dims) - 1 - axis_at))
    return loudness


def split_up(amount, total, reach, skew):
    portions = [(1 << 20) // math.isqrt(grade ** skew) + 1 for grade in range(2, amount + 1)]
    spare, holding = total - reach - (amount - 1), [1] * (amount - 1)
    while spare > 0:
        movable = [i for i in range(amount - 1) if holding[i] < reach]
        whole, budget = sum([portions[i] for i in movable]), spare
        for i in movable:
            addition = min(reach - holding[i], max(1, budget * portions[i] // whole), spare)
            holding[i] = holding[i] + addition
            spare = spare - addition
    return np.array([reach] + holding)


def uneven_parts(rng, amount, total, most, lean):
    if amount == 2:
        one = jax.random.randint(rng, (), max(1, total - most), min(most, total - 1) + 1)
        return jnp.stack([one, total - one])
    lengths = jnp.asarray(split_up(amount, total, most, lean), jnp.int32)
    couples = (amount - 1) // 2
    source_of, taker = lengths[1:1 + 2 * couples:2], lengths[2:2 + 2 * couples:2]
    slack = jnp.minimum(source_of - 1, most - taker)
    shifted = jax.random.randint(jax.random.fold_in(rng, 1), (couples,), 0, 1 << 20) % (slack + 1)
    lengths = lengths.at[1:1 + 2 * couples:2].set(source_of - shifted).at[2:2 + 2 * couples:2].set(taker + shifted)
    return lengths[jax.random.permutation(jax.random.fold_in(rng, 2), amount)]


def normal_values(rng, shape, scale, most, cuts=(), held_as=jnp.bfloat16):
    array = scale * jax.random.normal(rng, shape, jnp.float32)
    if cuts:
        array = array * level_of(rng, shape, cuts, -0.22, 0.18)
    return jnp.clip(array, -most, most).astype(held_as)


def bell_draw_with(own_key, extent, spread, reach, shards, heavy, held_as=jnp.bfloat16):
    array = spread * jax.random.normal(own_key, extent, jnp.float32)
    if shards:
        array = array * level_of(own_key, extent, shards, -0.22, 0.18)
    return jnp.clip(spiked(array, jax.random.fold_in(own_key, 3), *heavy), -reach, reach).astype(held_as)


def setup_inputs(seed: int = 0, part: int = 0) -> dict:
    arg_keys = jax.random.split(jax.random.key(seed), 8)
    part_keys = jax.random.split(jax.random.fold_in(arg_keys[7], part), 8)
    acts = normal_values(part_keys[0], (TOKENS, MODEL_WIDTH), 1.0, 6.0, ((0, 4), (1, 4)))
    output_weight = bell_draw_with(arg_keys[1], (MODEL_WIDTH, MODEL_WIDTH), MODEL_WIDTH ** -0.5, 0.09375, ((0, 4),), (0, 1, 4, 2.0))
    adapter_down_weight = normal_values(arg_keys[2], (ADAPTER_TOTAL, ADAPTER_RANK, MODEL_WIDTH), MODEL_WIDTH ** -0.5, 0.0625, ((0, 4), (2, 4)))
    adapter_up_weight = normal_values(arg_keys[3], (ADAPTER_TOTAL, ADAPTER_RANK, MODEL_WIDTH), ADAPTER_RANK ** -0.5, 1.5, ((0, 4), (2, 4)))
    segment_block_count = jax.vmap(lambda own: uneven_parts(own, GROUP_SEGMENTS, TOK // 16, MOST_BLOCKS, 2))(jax.random.split(part_keys[4], N_DP)).reshape((N_DP, GROUP_SEGMENTS)).astype(jnp.int32)
    segment_adapter_id = draw_segment_adapter_id(jax.random.fold_in(jax.random.fold_in(arg_keys[7], part), 71), part)
    adapter_store_row = draw_adapter_store_row(jax.random.fold_in(jax.random.fold_in(arg_keys[7], part), 71), part)
    return {"acts": acts, "output_weight": output_weight, "adapter_down_weight": adapter_down_weight, "adapter_up_weight": adapter_up_weight, "segment_block_count": segment_block_count, "segment_adapter_id": segment_adapter_id, "adapter_store_row": adapter_store_row}


adapter_scale = 0.5


def reference(acts, output_weight, adapter_down_weight, adapter_up_weight, segment_block_count, segment_adapter_id, adapter_store_row):
    width = MODEL_WIDTH // N_TENSOR

    def shard_term(carry, block):
        start = (block * width).astype(jnp.int32)
        columns = lax.dynamic_slice_in_dim(acts, start, width, 1)
        weights = lax.dynamic_slice_in_dim(output_weight, start, width, 0)
        partial_sum = jnp.dot(columns, weights, preferred_element_type=jnp.float32).astype(jnp.bfloat16)
        return carry + partial_sum.astype(jnp.float32), None

    base_output, _ = lax.scan(shard_term, jnp.zeros((TOKENS, MODEL_WIDTH), jnp.float32), jnp.arange(N_TENSOR, dtype=jnp.int32))
    ends = (jnp.cumsum(segment_block_count, axis=1) * 16).astype(jnp.int32)
    positions = jnp.arange(TOK, dtype=jnp.int32)
    rank_cols = jnp.arange(GROUP_SEGMENTS * ADAPTER_RANK, dtype=jnp.int32) // ADAPTER_RANK

    def group(index):
        start = (index * TOK).astype(jnp.int32)
        rows = lax.dynamic_slice_in_dim(acts, start, TOK, 0)
        segment = jnp.sum((positions[:, None] >= ends[index][None, :]).astype(jnp.int32), axis=1)
        within = segment[:, None] == rank_cols[None, :]
        stored_adapters = adapter_store_row[segment_adapter_id[index]]
        down_projected = adapter_down_weight[stored_adapters].reshape(GROUP_SEGMENTS * ADAPTER_RANK, MODEL_WIDTH)
        up_projected = adapter_up_weight[stored_adapters].reshape(GROUP_SEGMENTS * ADAPTER_RANK, MODEL_WIDTH)
        low = lax.dot_general(rows, down_projected, (((1,), (1,)), ((), ())), preferred_element_type=jnp.float32)
        low = jnp.where(within, low, jnp.zeros_like(low)).astype(jnp.bfloat16)
        return jnp.dot(low, up_projected, preferred_element_type=jnp.float32)

    adapter_delta = lax.map(group, jnp.arange(N_DP, dtype=jnp.int32)).reshape(TOKENS, MODEL_WIDTH)
    return (base_output + adapter_scale * adapter_delta).astype(jnp.bfloat16)
```

```python
import functools

import jax
import jax.numpy as jnp
from jax import lax
from jax.experimental import pallas as pl
from jax.experimental.pallas import tpu as pltpu
from jax.sharding import PartitionSpec as P

RANK = 16
SEGMENTS = 16
BLOCK = 16
CORES = 2
LANES = 128
adapter_scale = 0.5
VMEM_LIMIT = 40 * 1024 * 1024

ANY = pl.BlockSpec(memory_space=pl.ANY)
SMEM = pl.BlockSpec(memory_space=pltpu.SMEM)


def cost(flops, size):
    return pl.CostEstimate(flops=int(flops), bytes_accessed=int(size), transcendentals=0)


def chunks_of(width):
    if width % 1024:
        return [(0, width)]
    unit = width // 8
    return [(0, unit), (unit, 3 * unit), (4 * unit, 4 * unit)]


def product(place, acts, weight, shift, same_core, start, width, chips, add=None, after=()):
    rows, depth = acts.shape
    block = weight.shape[1] // (chips * CORES)
    tile = next(t for t in (256, 128) if start % t == 0 and width % t == 0)
    stride, first = block // tile, start // tile

    def columns(j, place_ref):
        core = place_ref[1] if same_core else 1 - place_ref[1]
        chip = lax.rem(place_ref[0] + shift, chips)
        return (0, (chip * CORES + core) * stride + first + j)

    def kernel(*refs):
        acts_ref, weight_ref = refs[1], refs[2]
        total = jnp.dot(acts_ref[...], weight_ref[...], preferred_element_type=jnp.float32)
        if add is not None:
            total = total + refs[3][...].astype(jnp.float32)
        refs[-1][...] = total.astype(jnp.bfloat16)

    operands = [acts, weight]
    specs = [pl.BlockSpec((rows, depth), lambda j, p: (0, 0)), pl.BlockSpec((depth, tile), columns)]
    if add is not None:
        operands.append(add)
        specs.append(pl.BlockSpec((rows, tile), lambda j, p: (0, j)))
    operands += list(after)
    specs += [ANY] * len(after)
    return pl.pallas_call(
        kernel,
        grid_spec=pltpu.PrefetchScalarGridSpec(
            num_scalar_prefetch=1,
            grid=(width // tile,),
            in_specs=specs,
            out_specs=pl.BlockSpec((rows, tile), lambda j, p: (0, j)),
        ),
        out_shape=jax.ShapeDtypeStruct((rows, width), jnp.bfloat16),
        compiler_params=pltpu.CompilerParams(vmem_limit_bytes=VMEM_LIMIT),
        cost_estimate=cost(2 * rows * depth * width, 2 * (rows * depth + depth * width + 2 * rows * width)),
    )(place, *operands)


def pick(ids, store_row, down, up, ways, cap, after=()):
    per_owner, rank, width = down.shape
    n_after = len(after)

    def kernel(*refs):
        id_refs, row_ref = refs[:ways], refs[ways]
        stores = refs[ways + 1 : ways + 3]
        outs = refs[ways + 3 + n_after : -2]
        slots, sems = refs[-2:]
        me = lax.axis_index("dp")
        for s in range(ways):
            for k in range(cap + 1):
                slots[s * (cap + 1) + k] = 0
            used = jnp.int32(0)
            for j in range(SEGMENTS):
                row = row_ref[id_refs[s][0, j]]
                local = row - me * per_owner
                mine = jnp.logical_and(local >= 0, local < per_owner)
                place = s * (cap + 1) + jnp.where(mine, jnp.minimum(used, cap), cap)
                slots[place] = jnp.where(mine, local, 0)
                used = used + mine.astype(jnp.int32)
        for which in range(2):
            for s in range(ways):
                out = outs[which * ways + s]
                for k in range(cap):
                    pltpu.make_async_copy(
                        stores[which].at[slots[s * (cap + 1) + k]],
                        out.at[pl.ds(k * rank, rank)],
                        sems.at[which * ways + s],
                    ).start()
        for which in range(2):
            for s in range(ways):
                out = outs[which * ways + s]
                pltpu.make_async_copy(out, out, sems.at[which * ways + s]).wait()

    shape = jax.ShapeDtypeStruct((cap * rank, width), jnp.bfloat16)
    outs = pl.pallas_call(
        kernel,
        in_specs=[SMEM] * (ways + 1) + [ANY] * (2 + n_after),
        out_specs=[ANY] * (2 * ways),
        out_shape=[shape] * (2 * ways),
        scratch_shapes=[pltpu.SMEM((ways * (cap + 1),), jnp.int32), pltpu.SemaphoreType.DMA((2 * ways,))],
        cost_estimate=cost(0, 4 * 2 * ways * cap * rank * width),
    )(*ids, store_row, down, up, *after)
    return outs[:ways], outs[ways:]


def token_slots(shape, axis, counts_ref, id_ref, row_ref, ways, cap, per_owner):
    me = lax.axis_index("dp")
    position = lax.broadcasted_iota(jnp.int32, shape, axis)
    owners, slot, start = [], jnp.full(shape, -1, jnp.int32), jnp.int32(0)
    for j in range(SEGMENTS):
        owner = row_ref[id_ref[0, j]] // per_owner
        order = jnp.int32(0)
        for other in owners:
            order = order + (other == owner).astype(jnp.int32)
        owners.append(owner)
        mine = lax.rem(me - owner + ways, ways) * cap + order
        slot = jnp.where(position >= start, mine, slot)
        start = start + counts_ref[0, j] * BLOCK
    return slot


def low_parts(acts, downs, counts, ids, store_row, cap, per_owner):
    rows, depth = acts.shape
    ways = len(downs)
    wide = ways * cap * RANK

    def kernel(counts_ref, id_ref, row_ref, acts_ref, *refs):
        out_ref = refs[-1]
        slot = token_slots((1, rows), 1, counts_ref, id_ref, row_ref, ways, cap, per_owner)
        total = jnp.zeros((RANK, rows), jnp.float32)
        for s in range(ways):
            part = lax.dot_general(
                refs[s][...], acts_ref[...], (((1,), (1,)), ((), ())), preferred_element_type=jnp.float32
            )
            for k in range(cap):
                piece = part[k * RANK : (k + 1) * RANK, :]
                total = total + jnp.where(slot == s * cap + k, piece, 0.0)
        out_ref[...] = total

    whole = pl.BlockSpec(memory_space=pltpu.VMEM)
    return pl.pallas_call(
        kernel,
        in_specs=[SMEM] * 3 + [whole] * (1 + ways),
        out_specs=whole,
        out_shape=jax.ShapeDtypeStruct((RANK, rows), jnp.float32),
        compiler_params=pltpu.CompilerParams(vmem_limit_bytes=VMEM_LIMIT),
        cost_estimate=cost(2 * rows * depth * wide, 2 * (rows * depth + wide * depth)),
    )(counts, ids, store_row, acts, *downs)


def spread(low, counts, ids, store_row, ways, cap, per_owner):
    rows = low.shape[1]
    wide = ways * cap * RANK

    def kernel(counts_ref, id_ref, row_ref, low_ref, out_ref):
        slot = token_slots((1, rows), 1, counts_ref, id_ref, row_ref, ways, cap, per_owner)
        held = low_ref[...]
        for k in range(ways * cap):
            out_ref[k * RANK : (k + 1) * RANK, :] = jnp.where(slot == k, held, 0.0).astype(jnp.bfloat16)

    whole = pl.BlockSpec(memory_space=pltpu.VMEM)
    return pl.pallas_call(
        kernel,
        in_specs=[SMEM] * 3 + [whole],
        out_specs=whole,
        out_shape=jax.ShapeDtypeStruct((wide, rows), jnp.bfloat16),
        cost_estimate=cost(0, 2 * wide * rows),
    )(counts, ids, store_row, low)


def finish(out, bases, base_start, arrived, low, ups, start, width, full):
    wide, rows = low.shape
    tile = next(t for t in (256, 128) if start % t == 0 and width % t == 0)
    first = start // tile
    ways = len(ups)
    depth = ups[0].shape[0]

    def kernel(*refs):
        out_ref = refs[-1]
        low_ref, up_refs = refs[0], refs[1 : 1 + ways]
        total = refs[1 + ways][...].astype(jnp.float32)
        for ref in refs[2 + ways : 2 + ways + len(arrived)]:
            total = total + ref[...].astype(jnp.float32)
        delta = jnp.zeros((rows, tile), jnp.float32)
        for s in range(ways):
            delta = delta + lax.dot_general(
                low_ref[s * depth : (s + 1) * depth, :],
                up_refs[s][...],
                (((0,), (0,)), ((), ())),
                preferred_element_type=jnp.float32,
            )
        out_ref[...] = (total + adapter_scale * delta).astype(jnp.bfloat16)

    here = pl.BlockSpec((rows, tile), lambda j: (0, j))
    there = pl.BlockSpec((rows, tile), lambda j: (0, first + j))
    base_first = (start - base_start) // tile
    specs = [pl.BlockSpec((wide, rows), lambda j: (0, 0))]
    specs += [pl.BlockSpec((depth, tile), lambda j: (0, first + j))] * ways
    specs += [pl.BlockSpec((rows, tile), lambda j: (0, base_first + j))] + [here] * len(arrived)
    operands = [low, *ups, bases, *arrived]
    aliases = {}
    if out is not None:
        aliases = {len(operands): 0}
        operands.append(out)
        specs.append(ANY)
    return pl.pallas_call(
        kernel,
        grid=(width // tile,),
        in_specs=specs,
        out_specs=there,
        out_shape=jax.ShapeDtypeStruct((rows, full), jnp.bfloat16),
        input_output_aliases=aliases,
        compiler_params=pltpu.CompilerParams(vmem_limit_bytes=VMEM_LIMIT),
        cost_estimate=cost(2 * rows * wide * width, 2 * rows * width * (2 + len(arrived)) + 2 * wide * width),
    )(*operands)


def body(ways, chips, acts, weight, down, up, counts, ids, store_row):
    per_owner = down.shape[0]
    rows, depth = acts.shape
    block = weight.shape[1] // (chips * CORES)
    cap = SEGMENTS // ways + 1
    tensor = lax.axis_index("tensor")
    place = jnp.stack([tensor // CORES, lax.rem(tensor, CORES)]).astype(jnp.int32)

    def along_dp(array, shift):
        return lax.ppermute(array, "dp", [(i, (i + shift) % ways) for i in range(ways)])

    def to_core(array):
        return lax.ppermute(array, "tensor", [(i, i ^ 1) for i in range(chips * CORES)])

    def to_chip(array, shift):
        size = chips * CORES
        return lax.ppermute(array, "tensor", [(i, (i + CORES * shift) % size) for i in range(size)])

    mul = functools.partial(product, place, acts, weight, chips=chips)
    chunks = chunks_of(block)
    first = [(shift, start, width) for (start, width) in chunks for shift in range(1, chips)]

    all_ids = [ids] + [along_dp(ids, -s) for s in range(1, ways)]
    sent = mul(*[first[0][0], False, *first[0][1:]])
    crossed = to_core(sent)
    downs, ups = pick(all_ids, store_row, down, up, ways, cap, after=(sent,))
    far_downs = [downs[0]] + [along_dp(downs[s], s) for s in range(1, ways)]

    arrived = {}
    for n, (shift, start, width) in enumerate(first):
        after = (downs[0],) if n == 0 else ()
        summed = mul(shift, True, start, width, add=crossed, after=after)
        arrived[shift, start] = to_chip(summed, shift)
        if n + 1 < len(first):
            shift, start, width = first[n + 1]
            crossed = to_core(mul(shift, False, start, width, after=(summed,)))
    crossed = to_core(mul(0, False, 0, block, after=(summed,)))
    base = mul(0, True, 0, block, add=crossed)

    low = lax.psum(low_parts(acts, far_downs, counts, ids, store_row, cap, per_owner), "tensor")
    low = spread(low, counts, ids, store_row, ways, cap, per_owner)
    far_ups = [ups[0]]
    for s in range(1, ways):
        held, _ = lax.optimization_barrier((ups[s], far_downs[s]))
        far_ups.append(along_dp(held, s))

    out = None
    for start, width in chunks:
        terms = [arrived[shift, start] for shift in range(1, chips)]
        out = finish(out, base, 0, terms, low, far_ups, start, width, block)
    return out


def solution(mesh):
    in_specs = (
        P(("parts", "dp"), "tensor"),
        P("tensor", None),
        P("dp", None, "tensor"),
        P("dp", None, "tensor"),
        P(("parts", "dp"), None),
        P(("parts", "dp"), None),
        P("parts"),
    )
    out_specs = P(("parts", "dp"), "tensor")
    ways, chips = mesh.shape["dp"], mesh.shape["tensor"] // CORES
    return jax.shard_map(
        functools.partial(body, ways, chips), mesh=mesh, in_specs=in_specs, out_specs=out_specs, check_vma=False
    )
```

```python
import functools
import math

import jax
import jax.numpy as jnp
from jax import lax
from jax.experimental import pallas as pl
from jax.experimental.pallas import tpu as pltpu
from jax.sharding import PartitionSpec as P

RANK = 16
SEGMENTS = 16
BLOCK = 16
CORES = 2
LANES = 128
adapter_scale = 0.5
VMEM_LIMIT = 20 * 1024 * 1024

ANY = pl.BlockSpec(memory_space=pl.ANY)
SMEM = pl.BlockSpec(memory_space=pltpu.SMEM)
WHOLE = pl.BlockSpec(memory_space=pltpu.VMEM)
CHEAP = pl.CostEstimate(flops=1000, bytes_accessed=1000, transcendentals=0)
PARAMS = pltpu.CompilerParams(vmem_limit_bytes=VMEM_LIMIT)


def chunks_of(width):
    if width % 2048:
        return [(0, width)]
    unit = width // 8
    return [(0, 2 * unit), (2 * unit, 3 * unit), (5 * unit, 3 * unit)]


def tile_of(start, width):
    return next(t for t in (512, 384, 256, 128) if start % t == 0 and width % t == 0)


def product(place, acts, weight, shift, same_core, start, width, chips, add=None, after=(), into=None, total=None, at=0):
    rows, depth = acts.shape
    block = weight.shape[1] // (chips * CORES)
    tile = tile_of(math.gcd(start, at), width)
    stride, first = block // tile, start // tile

    def columns(j, place_ref):
        core = place_ref[1] if same_core else 1 - place_ref[1]
        chip = lax.rem(place_ref[0] + shift, chips)
        return (0, (chip * CORES + core) * stride + first + j)

    def kernel(*refs):
        acts_ref, weight_ref = refs[1], refs[2]
        value = jnp.dot(acts_ref[...], weight_ref[...], preferred_element_type=jnp.float32)
        if add is not None:
            value = value + refs[3][...].astype(jnp.float32)
        refs[-1][...] = value.astype(jnp.bfloat16)

    operands = [acts, weight]
    specs = [WHOLE, pl.BlockSpec((depth, tile), columns)]
    if add is not None:
        operands.append(add)
        specs.append(pl.BlockSpec((rows, tile), lambda j, p: (0, j)))
    aliases = {}
    if into is not None:
        aliases = {len(operands) + 1: 0}
        operands.append(into)
        specs.append(ANY)
    operands += list(after)
    specs += [ANY] * len(after)
    place_at = at // tile
    return pl.pallas_call(
        kernel,
        grid_spec=pltpu.PrefetchScalarGridSpec(
            num_scalar_prefetch=1,
            grid=(width // tile,),
            in_specs=specs,
            out_specs=pl.BlockSpec((rows, tile), lambda j, p: (0, place_at + j)),
        ),
        out_shape=jax.ShapeDtypeStruct((rows, total or width), jnp.bfloat16),
        input_output_aliases=aliases,
        compiler_params=PARAMS,
        cost_estimate=CHEAP,
    )(place, *operands)


def pick(ids, store_row, down, up, ways, cap, after=()):
    per_owner, rank, width = down.shape
    n_after = len(after)

    def kernel(*refs):
        id_refs, row_ref = refs[:ways], refs[ways]
        stores = refs[ways + 1 : ways + 3]
        outs = refs[ways + 3 + n_after : -2]
        slots, sems = refs[-2:]
        me = lax.axis_index("dp")
        for s in range(ways):
            for k in range(cap + 1):
                slots[s * (cap + 1) + k] = 0
            used = jnp.int32(0)
            for j in range(SEGMENTS):
                row = row_ref[id_refs[s][0, j]]
                local = row - me * per_owner
                mine = jnp.logical_and(local >= 0, local < per_owner)
                place = s * (cap + 1) + jnp.where(mine, jnp.minimum(used, cap), cap)
                slots[place] = jnp.where(mine, local, 0)
                used = used + mine.astype(jnp.int32)
        for which in range(2):
            for s in range(ways):
                out = outs[which * ways + s]
                for k in range(cap):
                    pltpu.make_async_copy(
                        stores[which].at[slots[s * (cap + 1) + k]],
                        out.at[pl.ds(k * rank, rank)],
                        sems.at[which * ways + s],
                    ).start()
        for which in range(2):
            for s in range(ways):
                out = outs[which * ways + s]
                pltpu.make_async_copy(out, out, sems.at[which * ways + s]).wait()

    shape = jax.ShapeDtypeStruct((cap * rank, width), jnp.bfloat16)
    outs = pl.pallas_call(
        kernel,
        in_specs=[SMEM] * (ways + 1) + [ANY] * (2 + n_after),
        out_specs=[WHOLE] * (2 * ways),
        out_shape=[shape] * (2 * ways),
        scratch_shapes=[pltpu.SMEM((ways * (cap + 1),), jnp.int32), pltpu.SemaphoreType.DMA((2 * ways,))],
        compiler_params=PARAMS,
        cost_estimate=CHEAP,
    )(*ids, store_row, down, up, *after)
    return outs[:ways], outs[ways:]


def slot_mask(shape, counts_ref, id_ref, row_ref, ways, cap, per_owner):
    me = lax.axis_index("dp")
    column = lax.broadcasted_iota(jnp.int32, (1, shape[1]), 1) // RANK
    first = jnp.zeros((1, shape[1]), jnp.int32)
    last, start, owners = first, jnp.int32(0), []
    for j in range(SEGMENTS):
        owner = row_ref[id_ref[0, j]] // per_owner
        order = jnp.int32(0)
        for other in owners:
            order = order + (other == owner).astype(jnp.int32)
        owners.append(owner)
        here = column == lax.rem(me - owner + ways, ways) * cap + order
        first = jnp.where(here, start, first)
        start = start + counts_ref[0, j] * BLOCK
        last = jnp.where(here, start, last)
    position = lax.broadcasted_iota(jnp.int32, shape, 0)
    return jnp.logical_and(position >= first, position < last)


def rank_of(wide):
    row = lax.broadcasted_iota(jnp.int32, (RANK, wide), 0)
    column = lax.broadcasted_iota(jnp.int32, (RANK, wide), 1)
    return (lax.rem(column, RANK) == row).astype(jnp.bfloat16)


def low_parts(acts, downs, counts, ids, store_row, cap, per_owner, after=()):
    rows = acts.shape[0]
    ways = len(downs)
    wide = ways * cap * RANK

    def kernel(counts_ref, id_ref, row_ref, acts_ref, *refs):
        mask = slot_mask((rows, wide), counts_ref, id_ref, row_ref, ways, cap, per_owner)
        blocks = jnp.concatenate([ref[...] for ref in refs[:ways]], axis=0)
        part = lax.dot_general(
            acts_ref[...], blocks, (((1,), (1,)), ((), ())), preferred_element_type=jnp.float32
        )
        part = jnp.where(mask, part, 0.0).astype(jnp.bfloat16)
        refs[-1][...] = lax.dot_general(
            rank_of(wide), part, (((1,), (1,)), ((), ())), preferred_element_type=jnp.float32
        )

    return pl.pallas_call(
        kernel,
        in_specs=[SMEM] * 3 + [WHOLE] * (1 + ways) + [ANY] * len(after),
        out_specs=WHOLE,
        out_shape=jax.ShapeDtypeStruct((RANK, rows), jnp.float32),
        compiler_params=PARAMS,
        cost_estimate=CHEAP,
    )(counts, ids, store_row, acts, *downs, *after)


def spread(parts, counts, ids, store_row, ways, cap, per_owner):
    rows = parts[0].shape[1]
    wide = ways * cap * RANK

    def kernel(counts_ref, id_ref, row_ref, *refs):
        mask = slot_mask((rows, wide), counts_ref, id_ref, row_ref, ways, cap, per_owner)
        low = refs[0][...]
        for ref in refs[1:-1]:
            low = low + ref[...]
        low = lax.dot_general(
            low.astype(jnp.bfloat16), rank_of(wide), (((0,), (0,)), ((), ())), preferred_element_type=jnp.float32
        )
        refs[-1][...] = jnp.where(mask, low, 0.0).astype(jnp.bfloat16)

    return pl.pallas_call(
        kernel,
        in_specs=[SMEM] * 3 + [WHOLE] * len(parts),
        out_specs=WHOLE,
        out_shape=jax.ShapeDtypeStruct((rows, wide), jnp.bfloat16),
        compiler_params=PARAMS,
        cost_estimate=CHEAP,
    )(counts, ids, store_row, *parts)


def finish(out, bases, base_start, arrived, low, ups, start, width, full):
    rows, wide = low.shape
    tile = tile_of(start, width)
    first = start // tile
    ways = len(ups)
    depth = ups[0].shape[0]

    def kernel(*refs):
        out_ref = refs[-1]
        low_ref, up_refs = refs[0], refs[1 : 1 + ways]
        total = refs[1 + ways][...].astype(jnp.float32)
        for ref in refs[2 + ways : 2 + ways + len(arrived)]:
            total = total + ref[...].astype(jnp.float32)
        blocks = jnp.concatenate([ref[...] for ref in up_refs], axis=0)
        delta = jnp.dot(low_ref[...], blocks, preferred_element_type=jnp.float32)
        out_ref[...] = (total + adapter_scale * delta).astype(jnp.bfloat16)

    here = pl.BlockSpec((rows, tile), lambda j: (0, j))
    there = pl.BlockSpec((rows, tile), lambda j: (0, first + j))
    base_first = (start - base_start) // tile
    specs = [WHOLE]
    specs += [pl.BlockSpec((depth, tile), lambda j: (0, first + j))] * ways
    specs += [pl.BlockSpec((rows, tile), lambda j: (0, base_first + j))] + [here] * len(arrived)
    operands = [low, *ups, bases, *arrived]
    aliases = {}
    if out is not None:
        aliases = {len(operands): 0}
        operands.append(out)
        specs.append(ANY)
    return pl.pallas_call(
        kernel,
        grid=(width // tile,),
        in_specs=specs,
        out_specs=there,
        out_shape=jax.ShapeDtypeStruct((rows, full), jnp.bfloat16),
        input_output_aliases=aliases,
        compiler_params=PARAMS,
        cost_estimate=CHEAP,
    )(*operands)


def body(ways, chips, acts, weight, down, up, counts, ids, store_row):
    per_owner = down.shape[0]
    rows, depth = acts.shape
    block = weight.shape[1] // (chips * CORES)
    cap = SEGMENTS // ways + 1
    tensor = lax.axis_index("tensor")
    place = jnp.stack([tensor // CORES, lax.rem(tensor, CORES)]).astype(jnp.int32)

    def along_dp(array, shift):
        return lax.ppermute(array, "dp", [(i, (i + shift) % ways) for i in range(ways)])

    def to_core(array):
        return lax.ppermute(array, "tensor", [(i, i ^ 1) for i in range(chips * CORES)])

    def to_chip(array, shift):
        size = chips * CORES
        return lax.ppermute(array, "tensor", [(i, (i + CORES * shift) % size) for i in range(size)])

    mul = functools.partial(product, place, acts, weight, chips=chips)
    head, *tail = chunks_of(block)
    rest = block - head[1]

    all_ids = [ids] + [along_dp(ids, -s) for s in range(1, ways)]
    sent = mul(1, False, *head)
    crossed = to_core(sent)
    downs, ups = pick(all_ids, store_row, down, up, ways, cap, after=(sent,))
    far_downs = [downs[0]] + [along_dp(downs[s], s) for s in range(1, ways)]

    heads, tails, last = [], [], downs[0]
    for shift in range(1, chips):
        if shift > 1:
            crossed = to_core(mul(shift, False, *head, after=(last,)))
        last = mul(shift, True, *head, add=crossed, after=(last,))
        heads.append(to_chip(last, shift))
    for shift in range(1, chips) if tail else ():
        crossed, into = [], None
        for start, width in tail:
            last = mul(shift, False, start, width, after=(last,))
            crossed.append(to_core(last))
        for (start, width), add in zip(tail, crossed):
            into = mul(shift, True, start, width, add=add, after=(last,), into=into, total=rest, at=start - head[1])
            last = into
        tails.append(to_chip(into, shift))

    last = mul(0, False, 0, block, after=(last, *heads))
    crossed = to_core(last)
    low = low_parts(acts, far_downs, counts, ids, store_row, cap, per_owner, after=(last,))
    far_ups = [ups[0]]
    for s in range(1, ways):
        held, _ = lax.optimization_barrier((ups[s], far_downs[s]))
        far_ups.append(along_dp(held, s))
    chip_low = low + to_core(low)
    lows = [chip_low] + [to_chip(chip_low, shift) for shift in range(1, chips)]
    base = mul(0, True, 0, block, add=crossed, after=(chip_low,))
    low = spread(lows, counts, ids, store_row, ways, cap, per_owner)

    out = finish(None, base, 0, heads, low, far_ups, *head, block)
    if tail:
        out = finish(out, base, 0, tails, low, far_ups, head[1], rest, block)
    return out


def solution(mesh):
    in_specs = (
        P(("parts", "dp"), "tensor"),
        P("tensor", None),
        P("dp", None, "tensor"),
        P("dp", None, "tensor"),
        P(("parts", "dp"), None),
        P(("parts", "dp"), None),
        P("parts"),
    )
    out_specs = P(("parts", "dp"), "tensor")
    ways, chips = mesh.shape["dp"], mesh.shape["tensor"] // CORES
    return jax.shard_map(
        functools.partial(body, ways, chips), mesh=mesh, in_specs=in_specs, out_specs=out_specs, check_vma=False
    )
```

```python
import functools
import math

import jax
import jax.numpy as jnp
from jax import lax
from jax.experimental import pallas as pl
from jax.experimental.pallas import tpu as pltpu
from jax.sharding import PartitionSpec as P

RANK = 16
SEGMENTS = 16
BLOCK = 16
CORES = 2
LANES = 128
adapter_scale = 0.5
VMEM_LIMIT = 42 * 1024 * 1024

ANY = pl.BlockSpec(memory_space=pl.ANY)
HBM = pl.BlockSpec(memory_space=pltpu.HBM)
SMEM = pl.BlockSpec(memory_space=pltpu.SMEM)
WHOLE = pl.BlockSpec(memory_space=pltpu.VMEM)
CHEAP = pl.CostEstimate(flops=1000, bytes_accessed=1000, transcendentals=0)

def weigh(us):
    return pl.CostEstimate(flops=int(us * 1.1e9) + 1000, bytes_accessed=1000, transcendentals=0)
PARAMS = pltpu.CompilerParams(vmem_limit_bytes=VMEM_LIMIT)


def chunks_of(width):
    if width % 2048:
        return (0, width), None
    half = 1024
    return (0, half), (half, width - half)


def tile_of(start, width):
    return next(t for t in (512, 256, 128) if start % t == 0 and width % t == 0)


def product(place, acts, weight, shift, same_core, start, width, chips, add=None, after=(), into=None, total=None, at=0, weight_of=CHEAP):
    rows, depth = acts.shape
    block = weight.shape[1] // (chips * CORES)
    tile = tile_of(math.gcd(start, at), width)
    stride, first = block // tile, start // tile

    def columns(j, place_ref):
        core = place_ref[1] if same_core else 1 - place_ref[1]
        chip = lax.rem(place_ref[0] + shift, chips)
        return (0, (chip * CORES + core) * stride + first + j)

    def kernel(*refs):
        acts_ref, weight_ref = refs[1], refs[2]
        value = jnp.dot(acts_ref[...], weight_ref[...], preferred_element_type=jnp.float32)
        if add is not None:
            value = value + refs[3][...].astype(jnp.float32)
        refs[-1][...] = value.astype(jnp.bfloat16)

    operands = [acts, weight]
    specs = [WHOLE, pl.BlockSpec((depth, tile), columns)]
    if add is not None:
        operands.append(add)
        specs.append(pl.BlockSpec((rows, tile), lambda j, p: (0, j)))
    aliases = {}
    if into is not None:
        aliases = {len(operands) + 1: 0}
        operands.append(into)
        specs.append(ANY)
    operands += list(after)
    specs += [ANY] * len(after)
    place_at = at // tile
    return pl.pallas_call(
        kernel,
        grid_spec=pltpu.PrefetchScalarGridSpec(
            num_scalar_prefetch=1,
            grid=(width // tile,),
            in_specs=specs,
            out_specs=pl.BlockSpec((rows, tile), lambda j, p: (0, place_at + j)),
        ),
        out_shape=jax.ShapeDtypeStruct((rows, total or width), jnp.bfloat16),
        input_output_aliases=aliases,
        compiler_params=PARAMS,
        cost_estimate=weight_of,
    )(place, *operands)


def pick(ids, store_row, down, up, ways, cap, after=()):
    per_owner, rank, width = down.shape
    n_after = len(after)

    def kernel(*refs):
        id_refs, row_ref = refs[:ways], refs[ways]
        stores = refs[ways + 1 : ways + 3]
        outs = refs[ways + 3 + n_after : -2]
        slots, sems = refs[-2:]
        me = lax.axis_index("dp")
        for s in range(ways):
            for k in range(cap + 1):
                slots[s * (cap + 1) + k] = 0
            used = jnp.int32(0)
            for j in range(SEGMENTS):
                row = row_ref[id_refs[s][0, j]]
                local = row - me * per_owner
                mine = jnp.logical_and(local >= 0, local < per_owner)
                place = s * (cap + 1) + jnp.where(mine, jnp.minimum(used, cap), cap)
                slots[place] = jnp.where(mine, local, 0)
                used = used + mine.astype(jnp.int32)
        for which in range(2):
            for s in range(ways):
                out = outs[which * ways + s]
                for k in range(cap):
                    pltpu.make_async_copy(
                        stores[which].at[slots[s * (cap + 1) + k]],
                        out.at[pl.ds(k * rank, rank)],
                        sems.at[which * ways + s],
                    ).start()
        for which in range(2):
            for s in range(ways):
                out = outs[which * ways + s]
                pltpu.make_async_copy(out, out, sems.at[which * ways + s]).wait()

    shape = jax.ShapeDtypeStruct((cap * rank, width), jnp.bfloat16)
    outs = pl.pallas_call(
        kernel,
        in_specs=[SMEM] * (ways + 1) + [HBM] * 2 + [ANY] * n_after,
        out_specs=[WHOLE] * (2 * ways),
        out_shape=[shape] * (2 * ways),
        scratch_shapes=[pltpu.SMEM((ways * (cap + 1),), jnp.int32), pltpu.SemaphoreType.DMA((2 * ways,))],
        compiler_params=PARAMS,
        cost_estimate=CHEAP,
    )(*ids, store_row, down, up, *after)
    return outs[:ways], outs[ways:]


def slot_mask(shape, counts_ref, id_ref, row_ref, ways, cap, per_owner):
    me = lax.axis_index("dp")
    column = lax.broadcasted_iota(jnp.int32, (1, shape[1]), 1) // RANK
    first = jnp.zeros((1, shape[1]), jnp.int32)
    last, start, owners = first, jnp.int32(0), []
    for j in range(SEGMENTS):
        owner = row_ref[id_ref[0, j]] // per_owner
        order = jnp.int32(0)
        for other in owners:
            order = order + (other == owner).astype(jnp.int32)
        owners.append(owner)
        here = column == lax.rem(me - owner + ways, ways) * cap + order
        first = jnp.where(here, start, first)
        start = start + counts_ref[0, j] * BLOCK
        last = jnp.where(here, start, last)
    position = lax.broadcasted_iota(jnp.int32, shape, 0)
    return jnp.logical_and(position >= first, position < last)


def rank_of(wide):
    row = lax.broadcasted_iota(jnp.int32, (RANK, wide), 0)
    column = lax.broadcasted_iota(jnp.int32, (RANK, wide), 1)
    return (lax.rem(column, RANK) == row).astype(jnp.bfloat16)


def low_parts(acts, downs, counts, ids, store_row, cap, per_owner, after=()):
    rows = acts.shape[0]
    ways = len(downs)
    wide = ways * cap * RANK

    def kernel(counts_ref, id_ref, row_ref, acts_ref, *refs):
        mask = slot_mask((rows, wide), counts_ref, id_ref, row_ref, ways, cap, per_owner)
        blocks = jnp.concatenate([ref[...] for ref in refs[:ways]], axis=0)
        part = lax.dot_general(
            acts_ref[...], blocks, (((1,), (1,)), ((), ())), preferred_element_type=jnp.float32
        )
        part = jnp.where(mask, part, 0.0).astype(jnp.bfloat16)
        refs[-1][...] = lax.dot_general(
            rank_of(wide), part, (((1,), (1,)), ((), ())), preferred_element_type=jnp.float32
        )

    return pl.pallas_call(
        kernel,
        in_specs=[SMEM] * 3 + [WHOLE] * (1 + ways) + [ANY] * len(after),
        out_specs=WHOLE,
        out_shape=jax.ShapeDtypeStruct((RANK, rows), jnp.float32),
        compiler_params=PARAMS,
        cost_estimate=weigh(3),
    )(counts, ids, store_row, acts, *downs, *after)


def spread(parts, counts, ids, store_row, ways, cap, per_owner):
    rows = parts[0].shape[1]
    wide = ways * cap * RANK

    def kernel(counts_ref, id_ref, row_ref, *refs):
        mask = slot_mask((rows, wide), counts_ref, id_ref, row_ref, ways, cap, per_owner)
        low = refs[0][...]
        for ref in refs[1:-1]:
            low = low + ref[...]
        low = lax.dot_general(
            low.astype(jnp.bfloat16), rank_of(wide), (((0,), (0,)), ((), ())), preferred_element_type=jnp.float32
        )
        refs[-1][...] = jnp.where(mask, low, 0.0).astype(jnp.bfloat16)

    return pl.pallas_call(
        kernel,
        in_specs=[SMEM] * 3 + [WHOLE] * len(parts),
        out_specs=WHOLE,
        out_shape=jax.ShapeDtypeStruct((rows, wide), jnp.bfloat16),
        compiler_params=PARAMS,
        cost_estimate=weigh(1),
    )(counts, ids, store_row, *parts)


def finish(out, bases, base_start, arrived, low, ups, start, width, full):
    rows, wide = low.shape
    tile = tile_of(start, width)
    first = start // tile
    ways = len(ups)
    depth = ups[0].shape[0]

    def kernel(*refs):
        out_ref = refs[-1]
        low_ref, up_refs = refs[0], refs[1 : 1 + ways]
        total = refs[1 + ways][...].astype(jnp.float32)
        for ref in refs[2 + ways : 2 + ways + len(arrived)]:
            total = total + ref[...].astype(jnp.float32)
        blocks = jnp.concatenate([ref[...] for ref in up_refs], axis=0)
        delta = jnp.dot(low_ref[...], blocks, preferred_element_type=jnp.float32)
        out_ref[...] = (total + adapter_scale * delta).astype(jnp.bfloat16)

    here = pl.BlockSpec((rows, tile), lambda j: (0, j))
    there = pl.BlockSpec((rows, tile), lambda j: (0, first + j))
    base_first = (start - base_start) // tile
    specs = [WHOLE]
    specs += [pl.BlockSpec((depth, tile), lambda j: (0, first + j))] * ways
    specs += [pl.BlockSpec((rows, tile), lambda j: (0, base_first + j))] + [here] * len(arrived)
    operands = [low, *ups, bases, *arrived]
    aliases = {}
    if out is not None:
        aliases = {len(operands): 0}
        operands.append(out)
        specs.append(ANY)
    return pl.pallas_call(
        kernel,
        grid=(width // tile,),
        in_specs=specs,
        out_specs=there,
        out_shape=jax.ShapeDtypeStruct((rows, full), jnp.bfloat16),
        input_output_aliases=aliases,
        compiler_params=PARAMS,
        cost_estimate=weigh(8 if out is None else 1),
    )(*operands)


def apart(live, function, *operands):
    shapes = jax.eval_shape(function, *operands)
    return lax.cond(live, function, lambda *_: jax.tree.map(lambda t: jnp.zeros(t.shape, t.dtype), shapes), *operands)


def body(ways, chips, acts, weight, down, up, counts, ids, store_row):
    per_owner = down.shape[0]
    rows, depth = acts.shape
    block = weight.shape[1] // (chips * CORES)
    cap = SEGMENTS // ways + 1
    tensor = lax.axis_index("tensor")
    place = jnp.stack([tensor // CORES, lax.rem(tensor, CORES)]).astype(jnp.int32)

    def along_dp(array, shift):
        return lax.ppermute(array, "dp", [(i, (i + shift) % ways) for i in range(ways)])

    def to_core(array):
        return lax.ppermute(array, "tensor", [(i, i ^ 1) for i in range(chips * CORES)])

    def to_chip(array, shift):
        size = chips * CORES
        return lax.ppermute(array, "tensor", [(i, (i + CORES * shift) % size) for i in range(size)])

    mul = functools.partial(product, place, acts, weight, chips=chips)
    head, tail = chunks_of(block)

    all_ids = [ids] + [along_dp(ids, -s) for s in range(1, ways)]
    sent = mul(1, False, *head)
    crossed = to_core(sent)
    downs, ups = pick(all_ids, store_row, down, up, ways, cap, after=(sent,))
    far_downs = [downs[0]] + [along_dp(downs[s], s) for s in range(1, ways)]

    heads, tails, last = [], [], downs[0]
    for shift in range(1, chips):
        if shift > 1:
            crossed = to_core(mul(shift, False, *head, after=(last,)))
        last = mul(shift, True, *head, add=crossed, after=(last,))
        heads.append(to_chip(last, shift))

    live = counts[0, 0] >= 0

    def sums(acts, weight, place, last, shift, own):
        mul = functools.partial(product, place, acts, weight, chips=chips)
        last = mul(shift, False, *tail, after=(last,))
        crossed = to_core(last)
        if own:
            last = mul(0, False, 0, block, after=(last,))
            own_crossed = to_core(lax.optimization_barrier((last, crossed))[0])
        summed = mul(shift, True, *tail, add=crossed, after=(last,))
        return (summed, own_crossed) if own else (summed,)

    for shift in range(1, chips) if tail else ():
        own = shift == chips - 1
        last, *others = apart(live, functools.partial(sums, shift=shift, own=own), acts, weight, place, last)
        tails.append(to_chip(last, shift))
    own_crossed = others[0] if tail else to_core(mul(0, False, 0, block, after=(last,)))

    low = low_parts(acts, far_downs, counts, ids, store_row, cap, per_owner, after=(last, *heads))
    far_ups = [ups[0]]
    for s in range(1, ways):
        held, _, _ = lax.optimization_barrier((ups[s], far_downs[s], last))
        far_ups.append(along_dp(held, s))
    chip_low = low + to_core(low)
    lows = [chip_low] + [to_chip(chip_low, shift) for shift in range(1, chips)]
    base = mul(0, True, 0, block, add=own_crossed, after=(chip_low,), weight_of=weigh(0))
    low = spread(lows, counts, ids, store_row, ways, cap, per_owner)

    out = finish(None, base, 0, heads, low, far_ups, *head, block)
    if tail:
        out = finish(out, base, 0, tails, low, far_ups, *tail, block)
    return out


def solution(mesh):
    in_specs = (
        P(("parts", "dp"), "tensor"),
        P("tensor", None),
        P("dp", None, "tensor"),
        P("dp", None, "tensor"),
        P(("parts", "dp"), None),
        P(("parts", "dp"), None),
        P("parts"),
    )
    out_specs = P(("parts", "dp"), "tensor")
    ways, chips = mesh.shape["dp"], mesh.shape["tensor"] // CORES
    return jax.shard_map(
        functools.partial(body, ways, chips), mesh=mesh, in_specs=in_specs, out_specs=out_specs, check_vma=False
    )
```

```python
import functools
import math

import jax
import jax.numpy as jnp
from jax import lax
from jax.experimental import pallas as pl
from jax.experimental.pallas import tpu as pltpu
from jax.sharding import PartitionSpec as P

RANK = 16
SEGMENTS = 16
BLOCK = 16
CORES = 2
LANES = 128
adapter_scale = 0.5
VMEM_LIMIT = 42 * 1024 * 1024

ANY = pl.BlockSpec(memory_space=pl.ANY)
HBM = pl.BlockSpec(memory_space=pltpu.HBM)
SMEM = pl.BlockSpec(memory_space=pltpu.SMEM)
WHOLE = pl.BlockSpec(memory_space=pltpu.VMEM)
CHEAP = pl.CostEstimate(flops=1000, bytes_accessed=1000, transcendentals=0)

def weigh(us):
    return pl.CostEstimate(flops=int(us * 1.1e9) + 1000, bytes_accessed=1000, transcendentals=0)
PARAMS = pltpu.CompilerParams(vmem_limit_bytes=VMEM_LIMIT)


def chunks_of(width):
    if width % 2048:
        return (0, width), None
    half = 1024
    return (0, half), (half, width - half)


def tile_of(start, width):
    return next(t for t in (512, 256, 128) if start % t == 0 and width % t == 0)


def product(place, acts, weight, shift, same_core, start, width, chips, add=None, after=(), into=None, total=None, at=0, weight_of=CHEAP):
    rows, depth = acts.shape
    block = weight.shape[1] // (chips * CORES)
    tile = tile_of(math.gcd(start, at), width)
    stride, first = block // tile, start // tile

    def columns(j, place_ref):
        core = place_ref[1] if same_core else 1 - place_ref[1]
        chip = lax.rem(place_ref[0] + shift, chips)
        return (0, (chip * CORES + core) * stride + first + j)

    def kernel(*refs):
        acts_ref, weight_ref = refs[1], refs[2]
        value = jnp.dot(acts_ref[...], weight_ref[...], preferred_element_type=jnp.float32)
        if add is not None:
            value = value + refs[3][...].astype(jnp.float32)
        refs[-1][...] = value.astype(jnp.bfloat16)

    operands = [acts, weight]
    specs = [WHOLE, pl.BlockSpec((depth, tile), columns)]
    if add is not None:
        operands.append(add)
        specs.append(pl.BlockSpec((rows, tile), lambda j, p: (0, j)))
    aliases = {}
    if into is not None:
        aliases = {len(operands) + 1: 0}
        operands.append(into)
        specs.append(ANY)
    operands += list(after)
    specs += [ANY] * len(after)
    place_at = at // tile
    return pl.pallas_call(
        kernel,
        grid_spec=pltpu.PrefetchScalarGridSpec(
            num_scalar_prefetch=1,
            grid=(width // tile,),
            in_specs=specs,
            out_specs=pl.BlockSpec((rows, tile), lambda j, p: (0, place_at + j)),
        ),
        out_shape=jax.ShapeDtypeStruct((rows, total or width), jnp.bfloat16),
        input_output_aliases=aliases,
        compiler_params=PARAMS,
        cost_estimate=weight_of,
    )(place, *operands)


def pick(ids, store_row, stores, ways, cap, after=()):
    per_owner, rank, width = stores[0].shape
    n_after, n_stores = len(after), len(stores)

    def kernel(*refs):
        id_refs, row_ref = refs[:ways], refs[ways]
        store_refs = refs[ways + 1 : ways + 1 + n_stores]
        outs, sems = refs[ways + 1 + n_stores + n_after : -1], refs[-1]
        me = lax.axis_index("dp")
        for s in range(ways):
            used, chosen = jnp.int32(0), [jnp.int32(0)] * cap
            for j in range(SEGMENTS):
                local = row_ref[id_refs[s][0, j]] - me * per_owner
                mine = jnp.logical_and(local >= 0, local < per_owner)
                for k in range(min(cap, j + 1)):
                    chosen[k] = jnp.where(jnp.logical_and(mine, used == k), local, chosen[k])
                used = used + mine.astype(jnp.int32)
            for which in range(n_stores):
                for k in range(cap):
                    pltpu.make_async_copy(
                        store_refs[which].at[chosen[k]],
                        outs[which * ways + s].at[pl.ds(k * rank, rank)],
                        sems.at[which * ways + s],
                    ).start()
        for which in range(n_stores):
            for s in range(ways):
                out = outs[which * ways + s]
                pltpu.make_async_copy(out, out, sems.at[which * ways + s]).wait()

    shape = jax.ShapeDtypeStruct((cap * rank, width), jnp.bfloat16)
    outs = pl.pallas_call(
        kernel,
        in_specs=[SMEM] * (ways + 1) + [HBM] * n_stores + [ANY] * n_after,
        out_specs=[WHOLE] * (n_stores * ways),
        out_shape=[shape] * (n_stores * ways),
        scratch_shapes=[pltpu.SemaphoreType.DMA((n_stores * ways,))],
        compiler_params=PARAMS,
        cost_estimate=CHEAP,
    )(*ids, store_row, *stores, *after)
    return outs


def slot_mask(shape, counts_ref, id_ref, row_ref, ways, cap, per_owner):
    me = lax.axis_index("dp")
    column = lax.broadcasted_iota(jnp.int32, (1, shape[1]), 1) // RANK
    first = jnp.zeros((1, shape[1]), jnp.int32)
    last, start, owners = first, jnp.int32(0), []
    for j in range(SEGMENTS):
        owner = row_ref[id_ref[0, j]] // per_owner
        order = jnp.int32(0)
        for other in owners:
            order = order + (other == owner).astype(jnp.int32)
        owners.append(owner)
        here = column == lax.rem(me - owner + ways, ways) * cap + order
        first = jnp.where(here, start, first)
        start = start + counts_ref[0, j] * BLOCK
        last = jnp.where(here, start, last)
    position = lax.broadcasted_iota(jnp.int32, shape, 0)
    return jnp.logical_and(position >= first, position < last)


def rank_of(wide):
    row = lax.broadcasted_iota(jnp.int32, (RANK, wide), 0)
    column = lax.broadcasted_iota(jnp.int32, (RANK, wide), 1)
    return (lax.rem(column, RANK) == row).astype(jnp.bfloat16)


def low_parts(acts, downs, counts, ids, store_row, cap, per_owner, after=()):
    rows = acts.shape[0]
    ways = len(downs)
    wide = ways * cap * RANK

    def kernel(counts_ref, id_ref, row_ref, acts_ref, *refs):
        mask = slot_mask((rows, wide), counts_ref, id_ref, row_ref, ways, cap, per_owner)
        blocks = jnp.concatenate([ref[...] for ref in refs[:ways]], axis=0)
        part = lax.dot_general(
            acts_ref[...], blocks, (((1,), (1,)), ((), ())), preferred_element_type=jnp.float32
        )
        part = jnp.where(mask, part, 0.0).astype(jnp.bfloat16)
        refs[-1][...] = lax.dot_general(
            rank_of(wide), part, (((1,), (1,)), ((), ())), preferred_element_type=jnp.float32
        )

    return pl.pallas_call(
        kernel,
        in_specs=[SMEM] * 3 + [WHOLE] * (1 + ways) + [ANY] * len(after),
        out_specs=WHOLE,
        out_shape=jax.ShapeDtypeStruct((RANK, rows), jnp.float32),
        compiler_params=PARAMS,
        cost_estimate=weigh(20),
    )(counts, ids, store_row, acts, *downs, *after)


def finish(lows, ups, base, sends, counts, ids, store_row, cap, per_owner):
    rows, block = base.shape
    ways, depth = len(ups), ups[0].shape[0]
    wide = ways * depth
    tile = math.gcd(*[send[0].shape[1] for send in sends], 512)
    n_low = len(lows)

    def kernel(counts_ref, id_ref, row_ref, *refs):
        low_refs, up_refs = refs[:n_low], refs[n_low : n_low + ways][::-1]
        base_ref, *sent_refs = refs[n_low + ways : -2]
        out_ref, low_ref = refs[-2:]
        step = pl.program_id(0)

        @pl.when(step == 0)
        def _():
            mask = slot_mask((rows, wide), counts_ref, id_ref, row_ref, ways, cap, per_owner)
            low = low_refs[0][...]
            for ref in low_refs[1:]:
                low = low + ref[...]
            low = lax.dot_general(
                low.astype(jnp.bfloat16), rank_of(wide), (((0,), (0,)), ((), ())), preferred_element_type=jnp.float32
            )
            low_ref[...] = jnp.where(mask, low, 0.0).astype(jnp.bfloat16)

        def write(arrived):
            blocks = jnp.concatenate([ref[...] for ref in up_refs], axis=0)
            delta = jnp.dot(low_ref[...], blocks, preferred_element_type=jnp.float32)
            total = base_ref[...].astype(jnp.float32)
            for ref in arrived:
                total = total + ref[...].astype(jnp.float32)
            out_ref[...] = (total + adapter_scale * delta).astype(jnp.bfloat16)

        first, at = 0, 0
        for send in sends:
            steps, arrived = send[0].shape[1] // tile, sent_refs[at : at + len(send)]
            pl.when(jnp.logical_and(step >= first, step < first + steps))(functools.partial(write, arrived))
            first, at = first + steps, at + len(send)

    here = pl.BlockSpec((rows, tile), lambda j: (0, j))
    specs = [SMEM] * 3 + [WHOLE] * n_low + [pl.BlockSpec((depth, tile), lambda j: (0, j))] * ways + [here]
    first = 0
    for send in sends:
        steps = send[0].shape[1] // tile
        index = lambda j, first=first, steps=steps: (0, jnp.clip(j - first, 0, steps - 1))
        specs += [pl.BlockSpec((rows, tile), index)] * len(send)
        first += steps
    return pl.pallas_call(
        kernel,
        grid=(block // tile,),
        in_specs=specs,
        out_specs=here,
        out_shape=jax.ShapeDtypeStruct((rows, block), jnp.bfloat16),
        scratch_shapes=[pltpu.VMEM((rows, wide), jnp.bfloat16)],
        compiler_params=PARAMS,
        cost_estimate=CHEAP,
    )(counts, ids, store_row, *lows, *ups[::-1], base, *[array for send in sends for array in send])


def apart(live, function, *operands):
    shapes = jax.eval_shape(function, *operands)
    return lax.cond(live, function, lambda *_: jax.tree.map(lambda t: jnp.zeros(t.shape, t.dtype), shapes), *operands)


def body(ways, chips, acts, weight, down, up, counts, ids, store_row):
    per_owner = down.shape[0]
    rows, depth = acts.shape
    block = weight.shape[1] // (chips * CORES)
    cap = SEGMENTS // ways + 1
    tensor = lax.axis_index("tensor")
    place = jnp.stack([tensor // CORES, lax.rem(tensor, CORES)]).astype(jnp.int32)

    def along_dp(array, shift):
        return lax.ppermute(array, "dp", [(i, (i + shift) % ways) for i in range(ways)])

    def to_core(array):
        return lax.ppermute(array, "tensor", [(i, i ^ 1) for i in range(chips * CORES)])

    def to_chip(array, shift):
        size = chips * CORES
        return lax.ppermute(array, "tensor", [(i, (i + CORES * shift) % size) for i in range(size)])

    mul = functools.partial(product, place, acts, weight, chips=chips)
    head, tail = chunks_of(block)

    all_ids = [ids] + [along_dp(ids, -s) for s in range(1, ways)]
    sent = mul(1, False, *head)
    crossed = to_core(sent)
    heads, tails, last = [], [], sent
    for shift in range(1, chips):
        if shift > 1:
            crossed = to_core(mul(shift, False, *head, after=(last,)))
        last = mul(shift, True, *head, add=crossed)
        heads.append(to_chip(last, shift))
    downs = pick(all_ids, store_row, [down], ways, cap, after=(last,))
    far_downs = [downs[0]] + [along_dp(downs[s], s) for s in range(1, ways)]
    last = downs[0]

    live = counts[0, 0] >= 0

    def sums(acts, weight, place, last, shift, own):
        mul = functools.partial(product, place, acts, weight, chips=chips)
        last = mul(shift, False, *tail, after=(last,))
        crossed = to_core(last)
        if own:
            last = mul(0, False, 0, block, after=(last,))
            own_crossed = to_core(lax.optimization_barrier((last, crossed))[0])
        summed = mul(shift, True, *tail, add=crossed, after=(last,))
        return (summed, own_crossed) if own else (summed,)

    for shift in range(1, chips) if tail else ():
        own = shift == chips - 1
        last, *others = apart(live, functools.partial(sums, shift=shift, own=own), acts, weight, place, last)
        tails.append(to_chip(last, shift))
    own_crossed = others[0] if tail else to_core(mul(0, False, 0, block, after=(last,)))

    low = low_parts(acts, far_downs, counts, ids, store_row, cap, per_owner, after=(last, *heads))
    ups = pick(all_ids, store_row, [up], ways, cap, after=(last,))
    far_ups = [ups[0]]
    for s in range(1, ways):
        held, *_ = lax.optimization_barrier((ups[s], last, far_downs[s]))
        far_ups.append(along_dp(held, s))
    chip_low = low + to_core(low)
    lows = [chip_low] + [to_chip(chip_low, shift) for shift in range(1, chips)]
    base = mul(0, True, 0, block, add=own_crossed, after=(chip_low,), weight_of=weigh(0))
    sends = [heads, tails] if tail else [heads]
    return finish(lows, far_ups, base, sends, counts, ids, store_row, cap, per_owner)


def solution(mesh):
    in_specs = (
        P(("parts", "dp"), "tensor"),
        P("tensor", None),
        P("dp", None, "tensor"),
        P("dp", None, "tensor"),
        P(("parts", "dp"), None),
        P(("parts", "dp"), None),
        P("parts"),
    )
    out_specs = P(("parts", "dp"), "tensor")
    ways, chips = mesh.shape["dp"], mesh.shape["tensor"] // CORES
    return jax.shard_map(
        functools.partial(body, ways, chips), mesh=mesh, in_specs=in_specs, out_specs=out_specs, check_vma=False
    )
```

```python
import functools
import math

import jax
import jax.numpy as jnp
from jax import lax
from jax.experimental import pallas as pl
from jax.experimental.pallas import tpu as pltpu
from jax.sharding import PartitionSpec as P

RANK = 16
SEGMENTS = 16
BLOCK = 16
CORES = 2
LANES = 128
adapter_scale = 0.5
VMEM_LIMIT = 34 * 1024 * 1024

ANY = pl.BlockSpec(memory_space=pl.ANY)
HBM = pl.BlockSpec(memory_space=pltpu.HBM)
SMEM = pl.BlockSpec(memory_space=pltpu.SMEM)
WHOLE = pl.BlockSpec(memory_space=pltpu.VMEM)
CHEAP = pl.CostEstimate(flops=1000, bytes_accessed=1000, transcendentals=0)

def weigh(us):
    return pl.CostEstimate(flops=int(us * 1.1e9) + 1000, bytes_accessed=1000, transcendentals=0)
PARAMS = pltpu.CompilerParams(vmem_limit_bytes=VMEM_LIMIT)


def chunks_of(width):
    if width % 2048:
        return (0, width), None
    half = 1024
    return (0, half), (half, width - half)


def tile_of(start, width):
    return next(t for t in (512, 256, 128) if start % t == 0 and width % t == 0)


def product(place, acts, weight, shift, same_core, start, width, chips, add=None, after=(), into=None, total=None, at=0, weight_of=CHEAP):
    rows, depth = acts.shape
    block = weight.shape[1] // (chips * CORES)
    tile = tile_of(math.gcd(start, at), width)
    stride, first = block // tile, start // tile

    def columns(j, place_ref):
        core = place_ref[1] if same_core else 1 - place_ref[1]
        chip = lax.rem(place_ref[0] + shift, chips)
        return (0, (chip * CORES + core) * stride + first + j)

    def kernel(*refs):
        acts_ref, weight_ref = refs[1], refs[2]
        value = jnp.dot(acts_ref[...], weight_ref[...], preferred_element_type=jnp.float32)
        if add is not None:
            value = value + refs[3][...].astype(jnp.float32)
        refs[-1][...] = value.astype(jnp.bfloat16)

    operands = [acts, weight]
    specs = [WHOLE, pl.BlockSpec((depth, tile), columns)]
    if add is not None:
        operands.append(add)
        specs.append(pl.BlockSpec((rows, tile), lambda j, p: (0, j)))
    aliases = {}
    if into is not None:
        aliases = {len(operands) + 1: 0}
        operands.append(into)
        specs.append(ANY)
    operands += list(after)
    specs += [ANY] * len(after)
    place_at = at // tile
    return pl.pallas_call(
        kernel,
        grid_spec=pltpu.PrefetchScalarGridSpec(
            num_scalar_prefetch=1,
            grid=(width // tile,),
            in_specs=specs,
            out_specs=pl.BlockSpec((rows, tile), lambda j, p: (0, place_at + j)),
        ),
        out_shape=jax.ShapeDtypeStruct((rows, total or width), jnp.bfloat16),
        input_output_aliases=aliases,
        compiler_params=PARAMS,
        cost_estimate=weight_of,
    )(place, *operands)


def pick(ids, store_row, stores, ways, cap, after=()):
    per_owner, rank, width = stores[0].shape
    n_after, n_stores = len(after), len(stores)

    def kernel(*refs):
        id_refs, row_ref = refs[:ways], refs[ways]
        store_refs = refs[ways + 1 : ways + 1 + n_stores]
        outs, sems = refs[ways + 1 + n_stores + n_after : -1], refs[-1]
        me = lax.axis_index("dp")
        for s in range(ways):
            used, chosen = jnp.int32(0), [jnp.int32(0)] * cap
            for j in range(SEGMENTS):
                local = row_ref[id_refs[s][0, j]] - me * per_owner
                mine = jnp.logical_and(local >= 0, local < per_owner)
                for k in range(min(cap, j + 1)):
                    chosen[k] = jnp.where(jnp.logical_and(mine, used == k), local, chosen[k])
                used = used + mine.astype(jnp.int32)
            for which in range(n_stores):
                for k in range(cap):
                    pltpu.make_async_copy(
                        store_refs[which].at[chosen[k]],
                        outs[which * ways + s].at[pl.ds(k * rank, rank)],
                        sems.at[which * ways + s],
                    ).start()
        for which in range(n_stores):
            for s in range(ways):
                out = outs[which * ways + s]
                pltpu.make_async_copy(out, out, sems.at[which * ways + s]).wait()

    shape = jax.ShapeDtypeStruct((cap * rank, width), jnp.bfloat16)
    outs = pl.pallas_call(
        kernel,
        in_specs=[SMEM] * (ways + 1) + [HBM] * n_stores + [ANY] * n_after,
        out_specs=[WHOLE] * (n_stores * ways),
        out_shape=[shape] * (n_stores * ways),
        scratch_shapes=[pltpu.SemaphoreType.DMA((n_stores * ways,))],
        compiler_params=pltpu.CompilerParams(vmem_limit_bytes=50 * 1024 * 1024),
        cost_estimate=CHEAP,
    )(*ids, store_row, *stores, *after)
    return outs


def slot_mask(shape, counts_ref, id_ref, row_ref, ways, cap, per_owner):
    me = lax.axis_index("dp")
    column = lax.broadcasted_iota(jnp.int32, (1, shape[1]), 1) // RANK
    first = jnp.zeros((1, shape[1]), jnp.int32)
    last, start, owners = first, jnp.int32(0), []
    for j in range(SEGMENTS):
        owner = row_ref[id_ref[0, j]] // per_owner
        order = jnp.int32(0)
        for other in owners:
            order = order + (other == owner).astype(jnp.int32)
        owners.append(owner)
        here = column == lax.rem(me - owner + ways, ways) * cap + order
        first = jnp.where(here, start, first)
        start = start + counts_ref[0, j] * BLOCK
        last = jnp.where(here, start, last)
    position = lax.broadcasted_iota(jnp.int32, shape, 0)
    return jnp.logical_and(position >= first, position < last)


def rank_of(wide):
    row = lax.broadcasted_iota(jnp.int32, (RANK, wide), 0)
    column = lax.broadcasted_iota(jnp.int32, (RANK, wide), 1)
    return (lax.rem(column, RANK) == row).astype(jnp.bfloat16)


def low_parts(acts, downs, counts, ids, store_row, cap, per_owner, after=()):
    rows = acts.shape[0]
    ways = len(downs)
    wide = ways * cap * RANK

    def kernel(counts_ref, id_ref, row_ref, acts_ref, *refs):
        mask = slot_mask((rows, wide), counts_ref, id_ref, row_ref, ways, cap, per_owner)
        blocks = jnp.concatenate([ref[...] for ref in refs[:ways]], axis=0)
        part = lax.dot_general(
            acts_ref[...], blocks, (((1,), (1,)), ((), ())), preferred_element_type=jnp.float32
        )
        part = jnp.where(mask, part, 0.0).astype(jnp.bfloat16)
        refs[-1][...] = lax.dot_general(
            rank_of(wide), part, (((1,), (1,)), ((), ())), preferred_element_type=jnp.float32
        )

    return pl.pallas_call(
        kernel,
        in_specs=[SMEM] * 3 + [WHOLE] * (1 + ways) + [ANY] * len(after),
        out_specs=WHOLE,
        out_shape=jax.ShapeDtypeStruct((RANK, rows), jnp.float32),
        compiler_params=PARAMS,
        cost_estimate=weigh(20),
    )(counts, ids, store_row, acts, *downs, *after)


def finish(lows, ups, base, sends, counts, ids, store_row, cap, per_owner):
    rows, block = base.shape
    ways, depth = len(ups), ups[0].shape[0]
    wide = ways * depth
    tile = math.gcd(*[send[0].shape[1] for send in sends], 1024)
    n_low = len(lows)

    def kernel(counts_ref, id_ref, row_ref, *refs):
        low_refs, up_refs = refs[:n_low], refs[n_low : n_low + ways][::-1]
        base_ref, *sent_refs = refs[n_low + ways : -2]
        out_ref, low_ref = refs[-2:]
        step = pl.program_id(0)

        @pl.when(step == 0)
        def _():
            mask = slot_mask((rows, wide), counts_ref, id_ref, row_ref, ways, cap, per_owner)
            low = low_refs[0][...]
            for ref in low_refs[1:]:
                low = low + ref[...]
            low = lax.dot_general(
                low.astype(jnp.bfloat16), rank_of(wide), (((0,), (0,)), ((), ())), preferred_element_type=jnp.float32
            )
            low_ref[...] = jnp.where(mask, low, 0.0).astype(jnp.bfloat16)

        def write(arrived):
            blocks = jnp.concatenate([ref[...] for ref in up_refs], axis=0)
            delta = jnp.dot(low_ref[...], blocks, preferred_element_type=jnp.float32)
            total = base_ref[...].astype(jnp.float32)
            for ref in arrived:
                total = total + ref[...].astype(jnp.float32)
            out_ref[...] = (total + adapter_scale * delta).astype(jnp.bfloat16)

        first, at = 0, 0
        for send in sends:
            steps, arrived = send[0].shape[1] // tile, sent_refs[at : at + len(send)]
            pl.when(jnp.logical_and(step >= first, step < first + steps))(functools.partial(write, arrived))
            first, at = first + steps, at + len(send)

    here = pl.BlockSpec((rows, tile), lambda j: (0, j))
    specs = [SMEM] * 3 + [WHOLE] * n_low + [pl.BlockSpec((depth, tile), lambda j: (0, j))] * ways + [here]
    first = 0
    for send in sends:
        steps = send[0].shape[1] // tile
        index = lambda j, first=first, steps=steps: (0, jnp.clip(j - first, 0, steps - 1))
        specs += [pl.BlockSpec((rows, tile), index)] * len(send)
        first += steps
    return pl.pallas_call(
        kernel,
        grid=(block // tile,),
        in_specs=specs,
        out_specs=here,
        out_shape=jax.ShapeDtypeStruct((rows, block), jnp.bfloat16),
        scratch_shapes=[pltpu.VMEM((rows, wide), jnp.bfloat16)],
        compiler_params=PARAMS,
        cost_estimate=CHEAP,
    )(counts, ids, store_row, *lows, *ups[::-1], base, *[array for send in sends for array in send])


def apart(live, function, *operands):
    shapes = jax.eval_shape(function, *operands)
    return lax.cond(live, function, lambda *_: jax.tree.map(lambda t: jnp.zeros(t.shape, t.dtype), shapes), *operands)


def body(ways, chips, acts, weight, down, up, counts, ids, store_row):
    per_owner = down.shape[0]
    rows, depth = acts.shape
    block = weight.shape[1] // (chips * CORES)
    cap = SEGMENTS // ways + 1
    tensor = lax.axis_index("tensor")
    place = jnp.stack([tensor // CORES, lax.rem(tensor, CORES)]).astype(jnp.int32)

    def along_dp(array, shift):
        return lax.ppermute(array, "dp", [(i, (i + shift) % ways) for i in range(ways)])

    def to_core(array):
        return lax.ppermute(array, "tensor", [(i, i ^ 1) for i in range(chips * CORES)])

    def to_chip(array, shift):
        size = chips * CORES
        return lax.ppermute(array, "tensor", [(i, (i + CORES * shift) % size) for i in range(size)])

    mul = functools.partial(product, place, acts, weight, chips=chips)
    head, tail = chunks_of(block)

    all_ids = [ids] + [along_dp(ids, -s) for s in range(1, ways)]
    sent = mul(1, False, *head)
    crossed = to_core(sent)
    heads, tails, last = [], [], sent
    for shift in range(1, chips):
        if shift > 1:
            crossed = to_core(mul(shift, False, *head, after=(last,)))
        last = mul(shift, True, *head, add=crossed)
        heads.append(to_chip(last, shift))
    downs = pick(all_ids, store_row, [down], ways, cap, after=(last,))
    far_downs = [downs[0]] + [along_dp(downs[s], s) for s in range(1, ways)]
    last = downs[0]

    live = counts[0, 0] >= 0

    def sums(acts, weight, place, last, shift, own):
        mul = functools.partial(product, place, acts, weight, chips=chips)
        last = mul(shift, False, *tail, after=(last,))
        crossed = to_core(last)
        if own:
            last = mul(0, False, 0, block, after=(last,))
            own_crossed = to_core(lax.optimization_barrier((last, crossed))[0])
        summed = mul(shift, True, *tail, add=crossed, after=(last,))
        return (summed, own_crossed) if own else (summed,)

    for shift in range(1, chips) if tail else ():
        own = shift == chips - 1
        last, *others = apart(live, functools.partial(sums, shift=shift, own=own), acts, weight, place, last)
        tails.append(to_chip(last, shift))
    own_crossed = others[0] if tail else to_core(mul(0, False, 0, block, after=(last,)))

    low = low_parts(acts, far_downs, counts, ids, store_row, cap, per_owner, after=(last, *heads))
    ups = pick(all_ids, store_row, [up], ways, cap, after=(last,))
    far_ups = [ups[0]]
    for s in range(1, ways):
        held, *_ = lax.optimization_barrier((ups[s], last, far_downs[s]))
        far_ups.append(along_dp(held, s))
    chip_low = low + to_core(low)
    lows = [chip_low] + [to_chip(chip_low, shift) for shift in range(1, chips)]
    base = mul(0, True, 0, block, add=own_crossed, after=(chip_low,), weight_of=weigh(0))
    sends = [heads, tails] if tail else [heads]
    return finish(lows, far_ups, base, sends, counts, ids, store_row, cap, per_owner)


def solution(mesh):
    in_specs = (
        P(("parts", "dp"), "tensor"),
        P("tensor", None),
        P("dp", None, "tensor"),
        P("dp", None, "tensor"),
        P(("parts", "dp"), None),
        P(("parts", "dp"), None),
        P("parts"),
    )
    out_specs = P(("parts", "dp"), "tensor")
    ways, chips = mesh.shape["dp"], mesh.shape["tensor"] // CORES
    return jax.shard_map(
        functools.partial(body, ways, chips), mesh=mesh, in_specs=in_specs, out_specs=out_specs, check_vma=False
    )
```

```python
import functools
import math

import jax
import jax.numpy as jnp
from jax import lax
from jax.experimental import pallas as pl
from jax.experimental.pallas import tpu as pltpu
from jax.sharding import PartitionSpec as P

RANK = 16
SEGMENTS = 16
BLOCK = 16
CORES = 2
LANES = 128
adapter_scale = 0.5
VMEM_LIMIT = 34 * 1024 * 1024

ANY = pl.BlockSpec(memory_space=pl.ANY)
HBM = pl.BlockSpec(memory_space=pltpu.HBM)
SMEM = pl.BlockSpec(memory_space=pltpu.SMEM)
WHOLE = pl.BlockSpec(memory_space=pltpu.VMEM)
CHEAP = pl.CostEstimate(flops=1000, bytes_accessed=1000, transcendentals=0)

def weigh(us):
    return pl.CostEstimate(flops=int(us * 1.1e9) + 1000, bytes_accessed=1000, transcendentals=0)
PARAMS = pltpu.CompilerParams(vmem_limit_bytes=VMEM_LIMIT)


def chunks_of(width):
    if width % 2048:
        return (0, width), None
    half = 1024
    return (0, half), (half, width - half)


def tile_of(start, width):
    return next(t for t in (512, 256, 128) if start % t == 0 and width % t == 0)


def product(place, acts, weight, shift, same_core, start, width, chips, add=None, after=(), weight_of=CHEAP):
    rows, depth = acts.shape
    block = weight.shape[1] // (chips * CORES)
    adds = [] if add is None else [add]
    tile = tile_of(start, width)
    stride, first = block // tile, start // tile

    def columns(j, place_ref):
        core = place_ref[1] if same_core else 1 - place_ref[1]
        chip = lax.rem(place_ref[0] + shift, chips)
        return (0, (chip * CORES + core) * stride + first + j)

    def kernel(*refs):
        acts_ref, weight_ref = refs[1], refs[2]
        value = jnp.dot(acts_ref[...], weight_ref[...], preferred_element_type=jnp.float32)
        if adds:
            value = value + refs[3][...].astype(jnp.float32)
        refs[-1][...] = value.astype(jnp.bfloat16)

    operands = [acts, weight, *adds, *after]
    specs = [WHOLE, pl.BlockSpec((depth, tile), columns)]
    specs += [pl.BlockSpec((rows, tile), lambda j, p: (0, j))] * len(adds)
    specs += [ANY] * len(after)
    return pl.pallas_call(
        kernel,
        grid_spec=pltpu.PrefetchScalarGridSpec(
            num_scalar_prefetch=1,
            grid=(width // tile,),
            in_specs=specs,
            out_specs=pl.BlockSpec((rows, tile), lambda j, p: (0, j)),
        ),
        out_shape=jax.ShapeDtypeStruct((rows, width), jnp.bfloat16),
        compiler_params=PARAMS,
        cost_estimate=weight_of,
    )(place, *operands)


def pick(ids, store_row, stores, ways, cap, after=(), weight_of=CHEAP):
    per_owner, rank, width = stores[0].shape
    n_after, n_stores = len(after), len(stores)

    def kernel(*refs):
        id_refs, row_ref = refs[:ways], refs[ways]
        store_refs = refs[ways + 1 : ways + 1 + n_stores]
        outs, sems = refs[ways + 1 + n_stores + n_after : -1], refs[-1]
        me = lax.axis_index("dp")
        for s in range(ways):
            used, chosen = jnp.int32(0), [jnp.int32(0)] * cap
            for j in range(SEGMENTS):
                local = row_ref[id_refs[s][0, j]] - me * per_owner
                mine = jnp.logical_and(local >= 0, local < per_owner)
                for k in range(min(cap, j + 1)):
                    chosen[k] = jnp.where(jnp.logical_and(mine, used == k), local, chosen[k])
                used = used + mine.astype(jnp.int32)
            for which in range(n_stores):
                for k in range(cap):
                    pltpu.make_async_copy(
                        store_refs[which].at[chosen[k]],
                        outs[which * ways + s].at[pl.ds(k * rank, rank)],
                        sems.at[which * ways + s],
                    ).start()
        for which in range(n_stores):
            for s in range(ways):
                out = outs[which * ways + s]
                pltpu.make_async_copy(out, out, sems.at[which * ways + s]).wait()

    shape = jax.ShapeDtypeStruct((cap * rank, width), jnp.bfloat16)
    outs = pl.pallas_call(
        kernel,
        in_specs=[SMEM] * (ways + 1) + [HBM] * n_stores + [ANY] * n_after,
        out_specs=[WHOLE] * (n_stores * ways),
        out_shape=[shape] * (n_stores * ways),
        scratch_shapes=[pltpu.SemaphoreType.DMA((n_stores * ways,))],
        compiler_params=pltpu.CompilerParams(vmem_limit_bytes=50 * 1024 * 1024),
        cost_estimate=weight_of,
    )(*ids, store_row, *stores, *after)
    return outs


def slot_mask(shape, counts_ref, id_ref, row_ref, ways, cap, per_owner):
    me = lax.axis_index("dp")
    column = lax.broadcasted_iota(jnp.int32, (1, shape[1]), 1) // RANK
    first = jnp.zeros((1, shape[1]), jnp.int32)
    last, start, owners = first, jnp.int32(0), []
    for j in range(SEGMENTS):
        owner = row_ref[id_ref[0, j]] // per_owner
        order = jnp.int32(0)
        for other in owners:
            order = order + (other == owner).astype(jnp.int32)
        owners.append(owner)
        here = column == lax.rem(me - owner + ways, ways) * cap + order
        first = jnp.where(here, start, first)
        start = start + counts_ref[0, j] * BLOCK
        last = jnp.where(here, start, last)
    position = lax.broadcasted_iota(jnp.int32, shape, 0)
    return jnp.logical_and(position >= first, position < last)


def rank_of(wide):
    row = lax.broadcasted_iota(jnp.int32, (RANK, wide), 0)
    column = lax.broadcasted_iota(jnp.int32, (RANK, wide), 1)
    return (lax.rem(column, RANK) == row).astype(jnp.bfloat16)


def low_parts(acts, downs, counts, ids, store_row, cap, per_owner, after=()):
    rows = acts.shape[0]
    ways = len(downs)
    wide = ways * cap * RANK

    def kernel(counts_ref, id_ref, row_ref, acts_ref, *refs):
        mask = slot_mask((rows, wide), counts_ref, id_ref, row_ref, ways, cap, per_owner)
        blocks = jnp.concatenate([ref[...] for ref in refs[:ways]], axis=0)
        part = lax.dot_general(
            acts_ref[...], blocks, (((1,), (1,)), ((), ())), preferred_element_type=jnp.float32
        )
        part = jnp.where(mask, part, 0.0).astype(jnp.bfloat16)
        refs[-1][...] = lax.dot_general(
            rank_of(wide), part, (((1,), (1,)), ((), ())), preferred_element_type=jnp.float32
        )

    return pl.pallas_call(
        kernel,
        in_specs=[SMEM] * 3 + [WHOLE] * (1 + ways) + [ANY] * len(after),
        out_specs=WHOLE,
        out_shape=jax.ShapeDtypeStruct((RANK, rows), jnp.float32),
        compiler_params=PARAMS,
        cost_estimate=weigh(20),
    )(counts, ids, store_row, acts, *downs, *after)


def finish(lows, ups, sends, counts, ids, store_row, cap, per_owner):
    rows, block = lows[0].shape[1], sum(send[0].shape[1] for send in sends)
    ways, depth = len(ups), ups[0].shape[0]
    wide = ways * depth
    tile = math.gcd(*[send[0].shape[1] for send in sends], 1024)
    n_low = len(lows)

    def kernel(counts_ref, id_ref, row_ref, *refs):
        low_refs, up_refs = refs[:n_low], refs[n_low : n_low + ways][::-1]
        sent_refs = refs[n_low + ways : -2]
        out_ref, low_ref = refs[-2:]
        step = pl.program_id(0)

        @pl.when(step == 0)
        def _():
            mask = slot_mask((rows, wide), counts_ref, id_ref, row_ref, ways, cap, per_owner)
            low = low_refs[0][...]
            for ref in low_refs[1:]:
                low = low + ref[...]
            low = lax.dot_general(
                low.astype(jnp.bfloat16), rank_of(wide), (((0,), (0,)), ((), ())), preferred_element_type=jnp.float32
            )
            low_ref[...] = jnp.where(mask, low, 0.0).astype(jnp.bfloat16)

        def write(arrived):
            blocks = jnp.concatenate([ref[...] for ref in up_refs], axis=0)
            delta = jnp.dot(low_ref[...], blocks, preferred_element_type=jnp.float32)
            total = arrived[0][...].astype(jnp.float32)
            for ref in arrived[1:]:
                total = total + ref[...].astype(jnp.float32)
            out_ref[...] = (total + adapter_scale * delta).astype(jnp.bfloat16)

        first, at = 0, 0
        for send in sends:
            steps, arrived = send[0].shape[1] // tile, sent_refs[at : at + len(send)]
            pl.when(jnp.logical_and(step >= first, step < first + steps))(functools.partial(write, arrived))
            first, at = first + steps, at + len(send)

    here = pl.BlockSpec((rows, tile), lambda j: (0, j))
    specs = [SMEM] * 3 + [WHOLE] * n_low + [pl.BlockSpec((depth, tile), lambda j: (0, j))] * ways
    first = 0
    for send in sends:
        steps = send[0].shape[1] // tile
        index = lambda j, first=first, steps=steps: (0, jnp.clip(j - first, 0, steps - 1))
        specs += [pl.BlockSpec((rows, tile), index)] * len(send)
        first += steps
    return pl.pallas_call(
        kernel,
        grid=(block // tile,),
        in_specs=specs,
        out_specs=here,
        out_shape=jax.ShapeDtypeStruct((rows, block), jnp.bfloat16),
        scratch_shapes=[pltpu.VMEM((rows, wide), jnp.bfloat16)],
        compiler_params=PARAMS,
        cost_estimate=CHEAP,
    )(counts, ids, store_row, *lows, *ups[::-1], *[array for send in sends for array in send])


def apart(live, function, *operands):
    shapes = jax.eval_shape(function, *operands)
    return lax.cond(live, function, lambda *_: jax.tree.map(lambda t: jnp.zeros(t.shape, t.dtype), shapes), *operands)


def body(ways, chips, acts, weight, down, up, counts, ids, store_row):
    per_owner = down.shape[0]
    rows, depth = acts.shape
    block = weight.shape[1] // (chips * CORES)
    cap = SEGMENTS // ways + 1
    tensor = lax.axis_index("tensor")
    place = jnp.stack([tensor // CORES, lax.rem(tensor, CORES)]).astype(jnp.int32)

    def along_dp(array, shift):
        return lax.ppermute(array, "dp", [(i, (i + shift) % ways) for i in range(ways)])

    def to_core(array):
        return lax.ppermute(array, "tensor", [(i, i ^ 1) for i in range(chips * CORES)])

    def to_chip(array, shift):
        size = chips * CORES
        return lax.ppermute(array, "tensor", [(i, (i + CORES * shift) % size) for i in range(size)])

    mul = functools.partial(product, place, acts, weight, chips=chips)
    head, tail = chunks_of(block)

    all_ids = [ids] + [along_dp(ids, -s) for s in range(1, ways)]
    sent = mul(1, False, *head)
    crossed = to_core(sent)
    heads, tails, last = [], [], sent
    for shift in range(1, chips):
        if shift > 1:
            crossed = to_core(mul(shift, False, *head, after=(last,)))
        last = mul(shift, True, *head, add=crossed)
        heads.append(to_chip(last, shift))
    downs = pick(all_ids, store_row, [down], ways, cap, after=(last,))
    far_downs = [downs[0]] + [along_dp(downs[s], s) for s in range(1, ways)]
    last = downs[0]

    live = counts[0, 0] >= 0

    def sums(acts, weight, place, last, shift, own):
        mul = functools.partial(product, place, acts, weight, chips=chips)
        last = mul(shift, False, *tail, after=(last,))
        crossed = to_core(last)
        if own:
            last = mul(0, False, 0, block // 2, after=(last,))
            own_crossed = to_core(lax.optimization_barrier((last, crossed))[0])
        summed = mul(shift, True, *tail, add=crossed, after=(last,))
        return (summed, own_crossed) if own else (summed,)

    def rest(acts, weight, place, chip_low, crossed):
        mul = functools.partial(product, place, acts, weight, 0, chips=chips)
        half = block // 2
        last = mul(False, half, half, after=(chip_low,))
        second = to_core(last)
        first = mul(True, 0, half, add=crossed, after=(last,))
        lows = [to_chip(lax.optimization_barrier((chip_low, second, first))[0], shift) for shift in range(1, chips)]
        return first, mul(True, half, half, add=second, after=(first,)), *lows

    for shift in range(1, chips) if tail else ():
        own = shift == chips - 1
        last, *others = apart(live, functools.partial(sums, shift=shift, own=own), acts, weight, place, last)
        tails.append(to_chip(last, shift))
    ups = pick(all_ids, store_row, [up], ways, cap, after=(last,), weight_of=weigh(0))
    if not tail:
        others = [to_core(mul(0, False, 0, block, after=(last,)))]

    low = low_parts(acts, far_downs, counts, ids, store_row, cap, per_owner, after=(last, *heads))
    far_ups = [ups[0]]
    for s in range(1, ways):
        held, *_ = lax.optimization_barrier((ups[s], last, far_downs[s]))
        far_ups.append(along_dp(held, s))
    chip_low = low + to_core(low)
    if tail:
        first, second, *lows = apart(live, rest, acts, weight, place, chip_low, others[0])
        sends = [[first, *heads], [second, *tails]]
    else:
        lows = [to_chip(chip_low, shift) for shift in range(1, chips)]
        sends = [[mul(0, True, 0, block, add=others[0], after=(chip_low,)), *heads]]
    return finish([chip_low, *lows], far_ups, sends, counts, ids, store_row, cap, per_owner)


def solution(mesh):
    in_specs = (
        P(("parts", "dp"), "tensor"),
        P("tensor", None),
        P("dp", None, "tensor"),
        P("dp", None, "tensor"),
        P(("parts", "dp"), None),
        P(("parts", "dp"), None),
        P("parts"),
    )
    out_specs = P(("parts", "dp"), "tensor")
    ways, chips = mesh.shape["dp"], mesh.shape["tensor"] // CORES
    return jax.shard_map(
        functools.partial(body, ways, chips), mesh=mesh, in_specs=in_specs, out_specs=out_specs, check_vma=False
    )
```

```python
import functools
import math

import jax
import jax.numpy as jnp
from jax import lax
from jax.experimental import pallas as pl
from jax.experimental.pallas import tpu as pltpu
from jax.sharding import PartitionSpec as P

RANK = 16
SEGMENTS = 16
BLOCK = 16
CORES = 2
LANES = 128
adapter_scale = 0.5
VMEM_LIMIT = 34 * 1024 * 1024

ANY = pl.BlockSpec(memory_space=pl.ANY)
HBM = pl.BlockSpec(memory_space=pltpu.HBM)
SMEM = pl.BlockSpec(memory_space=pltpu.SMEM)
WHOLE = pl.BlockSpec(memory_space=pltpu.VMEM)
CHEAP = pl.CostEstimate(flops=1000, bytes_accessed=1000, transcendentals=0)

def weigh(us):
    return pl.CostEstimate(flops=int(us * 1.1e9) + 1000, bytes_accessed=1000, transcendentals=0)
PARAMS = pltpu.CompilerParams(vmem_limit_bytes=VMEM_LIMIT)


def chunks_of(width):
    if width % 2048:
        return (0, width), None
    half = 1024
    return (0, half), (half, width - half)


def tile_of(start, width):
    return next(t for t in (512, 256, 128) if start % t == 0 and width % t == 0)


def product(place, acts, weight, shift, same_core, start, width, chips, add=None, after=(), weight_of=CHEAP):
    rows, depth = acts.shape
    block = weight.shape[1] // (chips * CORES)
    adds = [] if add is None else [add]
    tile = tile_of(start, width)
    stride, first = block // tile, start // tile

    def columns(j, place_ref):
        core = place_ref[1] if same_core else 1 - place_ref[1]
        chip = lax.rem(place_ref[0] + shift, chips)
        return (0, (chip * CORES + core) * stride + first + j)

    def kernel(*refs):
        acts_ref, weight_ref = refs[1], refs[2]
        value = jnp.dot(acts_ref[...], weight_ref[...], preferred_element_type=jnp.float32)
        if adds:
            value = value + refs[3][...].astype(jnp.float32)
        refs[-1][...] = value.astype(jnp.bfloat16)

    operands = [acts, weight, *adds, *after]
    specs = [WHOLE, pl.BlockSpec((depth, tile), columns)]
    specs += [pl.BlockSpec((rows, tile), lambda j, p: (0, j))] * len(adds)
    specs += [ANY] * len(after)
    return pl.pallas_call(
        kernel,
        grid_spec=pltpu.PrefetchScalarGridSpec(
            num_scalar_prefetch=1,
            grid=(width // tile,),
            in_specs=specs,
            out_specs=pl.BlockSpec((rows, tile), lambda j, p: (0, j)),
        ),
        out_shape=jax.ShapeDtypeStruct((rows, width), jnp.bfloat16),
        compiler_params=PARAMS,
        cost_estimate=weight_of,
    )(place, *operands)


def pick(ids, store_row, stores, ways, cap, after=(), weight_of=CHEAP):
    per_owner, rank, width = stores[0].shape
    n_after, n_stores = len(after), len(stores)

    def kernel(*refs):
        id_refs, row_ref = refs[:ways], refs[ways]
        store_refs = refs[ways + 1 : ways + 1 + n_stores]
        outs, sems = refs[ways + 1 + n_stores + n_after : -1], refs[-1]
        me = lax.axis_index("dp")
        for s in range(ways):
            used, chosen = jnp.int32(0), [jnp.int32(0)] * cap
            for j in range(SEGMENTS):
                local = row_ref[id_refs[s][0, j]] - me * per_owner
                mine = jnp.logical_and(local >= 0, local < per_owner)
                for k in range(min(cap, j + 1)):
                    chosen[k] = jnp.where(jnp.logical_and(mine, used == k), local, chosen[k])
                used = used + mine.astype(jnp.int32)
            for which in range(n_stores):
                for k in range(cap):
                    pltpu.make_async_copy(
                        store_refs[which].at[chosen[k]],
                        outs[which * ways + s].at[pl.ds(k * rank, rank)],
                        sems.at[which * ways + s],
                    ).start()
        for which in range(n_stores):
            for s in range(ways):
                out = outs[which * ways + s]
                pltpu.make_async_copy(out, out, sems.at[which * ways + s]).wait()

    shape = jax.ShapeDtypeStruct((cap * rank, width), jnp.bfloat16)
    outs = pl.pallas_call(
        kernel,
        in_specs=[SMEM] * (ways + 1) + [HBM] * n_stores + [ANY] * n_after,
        out_specs=[WHOLE] * (n_stores * ways),
        out_shape=[shape] * (n_stores * ways),
        scratch_shapes=[pltpu.SemaphoreType.DMA((n_stores * ways,))],
        compiler_params=pltpu.CompilerParams(vmem_limit_bytes=50 * 1024 * 1024),
        cost_estimate=weight_of,
    )(*ids, store_row, *stores, *after)
    return outs


def slot_mask(shape, counts_ref, id_ref, row_ref, ways, cap, per_owner):
    me = lax.axis_index("dp")
    column = lax.broadcasted_iota(jnp.int32, (1, shape[1]), 1) // RANK
    first = jnp.zeros((1, shape[1]), jnp.int32)
    last, start, owners = first, jnp.int32(0), []
    for j in range(SEGMENTS):
        owner = row_ref[id_ref[0, j]] // per_owner
        order = jnp.int32(0)
        for other in owners:
            order = order + (other == owner).astype(jnp.int32)
        owners.append(owner)
        here = column == lax.rem(me - owner + ways, ways) * cap + order
        first = jnp.where(here, start, first)
        start = start + counts_ref[0, j] * BLOCK
        last = jnp.where(here, start, last)
    position = lax.broadcasted_iota(jnp.int32, shape, 0)
    return jnp.logical_and(position >= first, position < last)


def rank_of(wide):
    row = lax.broadcasted_iota(jnp.int32, (RANK, wide), 0)
    column = lax.broadcasted_iota(jnp.int32, (RANK, wide), 1)
    return (lax.rem(column, RANK) == row).astype(jnp.bfloat16)


def low_parts(acts, downs, counts, ids, store_row, cap, per_owner, after=()):
    rows = acts.shape[0]
    ways = len(downs)
    wide = ways * cap * RANK

    def kernel(counts_ref, id_ref, row_ref, acts_ref, *refs):
        mask = slot_mask((rows, wide), counts_ref, id_ref, row_ref, ways, cap, per_owner)
        blocks = jnp.concatenate([ref[...] for ref in refs[:ways]], axis=0)
        part = lax.dot_general(
            acts_ref[...], blocks, (((1,), (1,)), ((), ())), preferred_element_type=jnp.float32
        )
        part = jnp.where(mask, part, 0.0).astype(jnp.bfloat16)
        refs[-1][...] = lax.dot_general(
            rank_of(wide), part, (((1,), (1,)), ((), ())), preferred_element_type=jnp.float32
        )

    return pl.pallas_call(
        kernel,
        in_specs=[SMEM] * 3 + [WHOLE] * (1 + ways) + [ANY] * len(after),
        out_specs=WHOLE,
        out_shape=jax.ShapeDtypeStruct((RANK, rows), jnp.float32),
        compiler_params=PARAMS,
        cost_estimate=weigh(20),
    )(counts, ids, store_row, acts, *downs, *after)


def finish(lows, ups, sends, counts, ids, store_row, cap, per_owner):
    rows, block = lows[0].shape[1], sum(send[0].shape[1] for send in sends)
    ways, depth = len(ups), ups[0].shape[0]
    wide = ways * depth
    tile = math.gcd(*[send[0].shape[1] for send in sends], 1024)
    n_low = len(lows)

    def kernel(counts_ref, id_ref, row_ref, *refs):
        low_refs, up_refs = refs[:n_low], refs[n_low : n_low + ways]
        sent_refs = refs[n_low + ways : -2]
        out_ref, low_ref = refs[-2:]
        step = pl.program_id(0)

        @pl.when(step == 0)
        def _():
            mask = slot_mask((rows, wide), counts_ref, id_ref, row_ref, ways, cap, per_owner)
            low = low_refs[0][...]
            for ref in low_refs[1:]:
                low = low + ref[...]
            low = lax.dot_general(
                low.astype(jnp.bfloat16), rank_of(wide), (((0,), (0,)), ((), ())), preferred_element_type=jnp.float32
            )
            low_ref[...] = jnp.where(mask, low, 0.0).astype(jnp.bfloat16)

        def write(arrived):
            blocks = jnp.concatenate([ref[...] for ref in up_refs], axis=0)
            delta = jnp.dot(low_ref[...], blocks, preferred_element_type=jnp.float32)
            total = arrived[0][...].astype(jnp.float32)
            for ref in arrived[1:]:
                total = total + ref[...].astype(jnp.float32)
            out_ref[...] = (total + adapter_scale * delta).astype(jnp.bfloat16)

        first, at = 0, 0
        for send in sends:
            steps, arrived = send[0].shape[1] // tile, sent_refs[at : at + len(send)]
            pl.when(jnp.logical_and(step >= first, step < first + steps))(functools.partial(write, arrived))
            first, at = first + steps, at + len(send)

    here = pl.BlockSpec((rows, tile), lambda j: (0, j))
    specs = [SMEM] * 3 + [WHOLE] * n_low + [pl.BlockSpec((depth, tile), lambda j: (0, j))] * ways
    first = 0
    for send in sends:
        steps = send[0].shape[1] // tile
        index = lambda j, first=first, steps=steps: (0, jnp.clip(j - first, 0, steps - 1))
        specs += [pl.BlockSpec((rows, tile), index)] * len(send)
        first += steps
    return pl.pallas_call(
        kernel,
        grid=(block // tile,),
        in_specs=specs,
        out_specs=here,
        out_shape=jax.ShapeDtypeStruct((rows, block), jnp.bfloat16),
        scratch_shapes=[pltpu.VMEM((rows, wide), jnp.bfloat16)],
        compiler_params=PARAMS,
        cost_estimate=CHEAP,
    )(counts, ids, store_row, *lows, *ups, *[array for send in sends for array in send])


def apart(live, function, *operands):
    shapes = jax.eval_shape(function, *operands)
    return lax.cond(live, function, lambda *_: jax.tree.map(lambda t: jnp.zeros(t.shape, t.dtype), shapes), *operands)


def body(ways, chips, acts, weight, down, up, counts, ids, store_row):
    per_owner = down.shape[0]
    rows, depth = acts.shape
    block = weight.shape[1] // (chips * CORES)
    cap = SEGMENTS // ways + 1
    tensor = lax.axis_index("tensor")
    place = jnp.stack([tensor // CORES, lax.rem(tensor, CORES)]).astype(jnp.int32)

    def along_dp(array, shift):
        return lax.ppermute(array, "dp", [(i, (i + shift) % ways) for i in range(ways)])

    def to_core(array):
        return lax.ppermute(array, "tensor", [(i, i ^ 1) for i in range(chips * CORES)])

    def to_chip(array, shift):
        size = chips * CORES
        return lax.ppermute(array, "tensor", [(i, (i + CORES * shift) % size) for i in range(size)])

    mul = functools.partial(product, place, acts, weight, chips=chips)
    head, tail = chunks_of(block)

    all_ids = [ids] + [along_dp(ids, -s) for s in range(1, ways)]
    sent = mul(1, False, *head)
    crossed = to_core(sent)
    heads, tails, last = [], [], sent
    for shift in range(1, chips):
        if shift > 1:
            crossed = to_core(mul(shift, False, *head, after=(last,)))
        last = mul(shift, True, *head, add=crossed)
        heads.append(to_chip(last, shift))
    downs = pick(all_ids, store_row, [down], ways, cap, after=(last,))
    far_downs = [downs[0]] + [along_dp(downs[s], s) for s in range(1, ways)]
    last = downs[0]

    live = counts[0, 0] >= 0

    def sums(acts, weight, place, last, shift, own):
        mul = functools.partial(product, place, acts, weight, chips=chips)
        last = mul(shift, False, *tail, after=(last,))
        crossed = to_core(last)
        if own:
            last = mul(0, False, 0, block // 2, after=(last,))
            own_crossed = to_core(lax.optimization_barrier((last, crossed))[0])
        summed = mul(shift, True, *tail, add=crossed, after=(last,))
        return (summed, own_crossed) if own else (summed,)

    def rest(acts, weight, place, chip_low, crossed):
        mul = functools.partial(product, place, acts, weight, 0, chips=chips)
        half = block // 2
        last = mul(False, half, half, after=(chip_low,))
        second = to_core(last)
        first = mul(True, 0, half, add=crossed, after=(last,))
        lows = [to_chip(lax.optimization_barrier((chip_low, second, first))[0], shift) for shift in range(1, chips)]
        return first, mul(True, half, half, add=second, after=(first,)), *lows

    for shift in range(1, chips) if tail else ():
        own = shift == chips - 1
        last, *others = apart(live, functools.partial(sums, shift=shift, own=own), acts, weight, place, last)
        tails.append(to_chip(last, shift))
    ups = pick(all_ids, store_row, [up], ways, cap, after=(last,), weight_of=weigh(0))
    if not tail:
        others = [to_core(mul(0, False, 0, block, after=(last,)))]

    low = low_parts(acts, far_downs, counts, ids, store_row, cap, per_owner, after=(last, *heads))
    far_ups = [ups[0]]
    for s in range(1, ways):
        held, *_ = lax.optimization_barrier((ups[s], last, *far_downs[1:]))
        far_ups.append(along_dp(held, s))
    chip_low = low + to_core(low)
    if tail:
        first, second, *lows = apart(live, rest, acts, weight, place, chip_low, others[0])
        sends = [[first, *heads], [second, *tails]]
    else:
        lows = [to_chip(chip_low, shift) for shift in range(1, chips)]
        sends = [[mul(0, True, 0, block, add=others[0], after=(chip_low,)), *heads]]
    return finish([chip_low, *lows], far_ups, sends, counts, ids, store_row, cap, per_owner)


def solution(mesh):
    in_specs = (
        P(("parts", "dp"), "tensor"),
        P("tensor", None),
        P("dp", None, "tensor"),
        P("dp", None, "tensor"),
        P(("parts", "dp"), None),
        P(("parts", "dp"), None),
        P("parts"),
    )
    out_specs = P(("parts", "dp"), "tensor")
    ways, chips = mesh.shape["dp"], mesh.shape["tensor"] // CORES
    return jax.shard_map(
        functools.partial(body, ways, chips), mesh=mesh, in_specs=in_specs, out_specs=out_specs, check_vma=False
    )
```
